256 devices in a mesh: row: 16 (over x, z_lo, core), col: 16 (over z_hi, y).
Axes of the slice: x: 4, y: 4, z: 8 (z_hi: 4, z_lo: 2; z = z_hi * 2 + z_lo), core: 2. Of those that a mesh axis runs over, the one named last changes fastest.
Arguments:
- amps: bfloat16 [16, 16, 16, 4096], P('row', 'col'), may hold values from -6 to 6
- source: bfloat16 [16, 16, 16, 4096], P('row', 'col'), may hold values from -6 to 6
- factors: bfloat16 [16, 1024, 1024], P(None, ('row', 'col')), may hold values from -0.09375 to 0.09375
- screen: int32 [16, 8, 8], replicated, may hold values from 0 to 1, as said below
- occ_energy: float32 [4], replicated, may hold values from -1.5 to -0.3
- vir_energy: float32 [1024], replicated, may hold values from 0.2 to 2.5
Outputs:
- new_amps: bfloat16 [16, 16, 16, 4096], P('row', 'col')
The draws below stay inside these ranges and needn't reach their ends.
Inputs may be any that keep to these rules, and one draw needn't show every extreme that they name: screen[i * 4 + j, A, B] equals screen[j * 4 + i, B, A].
All inputs are finite; a program needn't handle non-finite values.
Results may differ from the reference program's by a relative error of at most 0.012.
Values may be sent and summed in bfloat16 or wider, within the bound.
No kernel may reach another device: no remote copies, remote signals or barrier semaphores. Data moves between devices by JAX's collectives and lax.ppermute only.
A program may use at most 192 MiB of HBM per device.

```python
import jax
import jax.numpy as jnp
from jax import lax

NO = 4
PAIRS = 16
VBLK = 128
NVB = 8
NV = 1024
NQ = 16
VG = 4
ALOC = 64
TILE = 4096
N_ROW = 16
N_COL = 16


def draw_screen(key, part):
    key = jax.random.fold_in(key, 11)
    raw_levels = jax.random.randint(key, (NO, NO, NVB, NVB), 0, 3)
    summed = raw_levels + jnp.transpose(raw_levels, (1, 0, 3, 2))
    return (summed >= 2).astype(jnp.int32).reshape(NO * NO, NVB, NVB)


def levels(stream_key, shape, cuts, smallest, top_value):
    factor_of = 1.0
    for position, shards_of in cuts:
        steps = jax.random.uniform(jax.random.fold_in(jax.random.fold_in(stream_key, 6), position), (shards_of,), jnp.float32, smallest / len(cuts), top_value / len(cuts))
        factor_of = factor_of * jnp.repeat(jnp.exp(steps), shape[position] // shards_of).reshape((-1,) + (1,) * (len(shape) - 1 - position))
    return factor_of


def scatter_about(key, extent, deviation, limit, split=(), dtype=jnp.bfloat16):
    result = deviation * jax.random.normal(key, extent, jnp.float32)
    if split:
        result = result * levels(key, extent, split, -0.22, 0.18)
    return jnp.clip(result, -limit, limit).astype(dtype)


def setup_inputs(seed: int = 0) -> dict:
    streams_of = jax.random.split(jax.random.key(seed), 7)
    amps = scatter_about(streams_of[0], (N_ROW, N_COL, PAIRS, TILE), 1.0, 6.0, ((0, 16), (1, 16)))
    source = scatter_about(streams_of[1], (N_ROW, N_COL, PAIRS, TILE), 1.0, 6.0, ((0, 16), (1, 16)))
    factors = scatter_about(streams_of[2], (NQ, NV, NV), (4 * NV) ** -0.5, 0.09375, ((1, 256),))
    screen = draw_screen(jax.random.fold_in(streams_of[6], 71), 0)
    occ_energy = jnp.clip(jax.random.uniform(streams_of[4], (NO,), jnp.float32, -1.5, -0.3), -1.5, -0.3)
    vir_energy = jnp.clip(jax.random.uniform(streams_of[5], (NV,), jnp.float32, 0.2, 2.5), 0.2, 2.5)
    return dict(amps=amps, source=source, factors=factors, screen=screen, occ_energy=occ_energy, vir_energy=vir_energy)


def to_dense(blocked):
    shaped = blocked.reshape(N_ROW, N_COL, PAIRS, ALOC, N_ROW, VG)
    return shaped.transpose(2, 0, 3, 4, 1, 5).reshape(PAIRS, NV, NV)


def to_blocked(dense):
    shaped = dense.reshape(PAIRS, N_ROW, ALOC, N_ROW, N_COL, VG)
    return shaped.transpose(1, 4, 0, 2, 3, 5).reshape(N_ROW, N_COL, PAIRS, TILE)


def reference(amps, source, factors, screen, occ_energy, vir_energy):
    dense_amps = to_dense(amps.astype(jnp.float32))
    dense_source = to_dense(source.astype(jnp.float32))
    block_of = jnp.arange(NV) // VBLK
    mask_full = screen.astype(jnp.float32)[:, block_of][:, :, block_of]
    screened = (dense_amps * mask_full).astype(jnp.bfloat16).astype(jnp.float32)
    factor_full = factors.astype(jnp.float32)

    def accumulate(aux_id, running):
        factor = factor_full[aux_id]
        inner_part = jnp.einsum('pcd,bd->pcb', screened, factor).astype(jnp.bfloat16)
        inner_part = lax.optimization_barrier(inner_part).astype(jnp.float32)
        return running + jnp.einsum('ac,pcb->pab', factor, inner_part)

    ladder = lax.fori_loop(0, NQ, accumulate, jnp.zeros((PAIRS, NV, NV), jnp.float32))
    resid = dense_source + ladder
    swapped = resid.reshape(NO, NO, NV, NV).transpose(1, 0, 3, 2).reshape(PAIRS, NV, NV)
    rsym = resid + swapped
    occ_pair = (occ_energy[:, None] + occ_energy[None, :]).reshape(PAIRS)
    denom = occ_pair[:, None, None] - vir_energy[None, :, None] - vir_energy[None, None, :]
    updated = mask_full * (dense_amps + rsym / denom)
    return to_blocked(updated.astype(jnp.bfloat16))
```

```python
import functools

import jax
import jax.numpy as jnp
import numpy as np
from jax import lax
from jax.experimental import pallas as pl
from jax.experimental.pallas import tpu as pltpu
from jax.sharding import Mesh
from jax.sharding import PartitionSpec as P

AXES = ("x", "zl", "core", "zh", "y")
PLANE = ("x", "y")
SLOTS = ("zh", "zl", "core")
PAIR_OF_SLOT = (1, 4, 2, 8, 3, 12, 6, 9, 7, 13, 11, 14, 0, 5, 10, 15)
N_OFF = 12
VMEM = pltpu.CompilerParams(vmem_limit_bytes=40 * 1024 * 1024)
F32 = jnp.float32
BF16 = jnp.bfloat16
NT = (((1,), (1,)), ((), ()))


def _one_hot(source_of):
    source_of = np.asarray(source_of).reshape(-1)
    size = source_of.size
    out = np.zeros((size, size), np.float32)
    out[np.arange(size), source_of] = 1
    return out


def _grid(*sizes):
    return np.meshgrid(*[np.arange(s) for s in sizes], indexing="ij")


def _tables():
    zc, j, h = _grid(4, 32, 2)
    rows_nat = _one_hot(zc * 64 + h * 32 + j)
    rb, zh, k = _grid(16, 4, 4)
    cols_rb = _one_hot(zh * 64 + rb * 4 + k).T
    ya, zc, zh, k = _grid(4, 4, 4, 4)
    a_loc = zh * 16 + ya * 4 + k
    rows_src = _one_hot(zc * 64 + (a_loc % 2) * 32 + a_loc // 2)
    x, zh, zc, k = _grid(4, 4, 4, 4)
    cols_src = _one_hot(zh * 64 + (x * 4 + zc) * 4 + k).T
    first = np.stack([rows_nat, cols_rb, rows_src, cols_src])
    zc, zh, y, k = _grid(4, 4, 4, 4)
    swap_a = _one_hot(((y * 4 + zh) * 4 + zc) * 4 + k)
    zh, x, zc, k = _grid(4, 4, 4, 4)
    swap_b = _one_hot(((x * 4 + zc) * 4 + zh) * 4 + k).T
    last = np.stack([swap_a, swap_b, rows_nat.T])
    y, x, zc, k = _grid(4, 4, 4, 4)
    rows_b = _one_hot(((zc * 4 + x) * 4 + y) * 4 + k)
    nat = np.zeros((2, 256, 512), np.float32)
    for parity in range(2):
        y, rl, zh, k = _grid(4, 4, 4, 4)
        nat[parity, rl * 64 + zh * 16 + y * 4 + k, y * 128 + (parity * 4 + rl) * 16 + zh * 4 + k] = 1
    return [np.asarray(t, jnp.bfloat16) for t in (first, last, rows_b, nat)]


def _perm(left, right):
    return jnp.dot(left, right, preferred_element_type=F32).astype(BF16)


def _mask_kernel(place_ref, amps_ref, source_ref, screen_ref, sent_ref, mask_ref, flat_ref):
    block = screen_ref[place_ref[0]].astype(F32)
    lane_block = (lax.broadcasted_iota(jnp.int32, (8, 128), 1) % 64) // 8
    spread = (lax.broadcasted_iota(jnp.int32, (8, 128), 0) == lane_block).astype(F32)
    mask = jnp.dot(block, spread, preferred_element_type=F32)
    mask_ref[...] = mask
    for first, ref in ((0, amps_ref), (32, source_ref)):
        for j in range(32):
            tile = ref[:, j * 128 : (j + 1) * 128].astype(F32)
            if first == 0:
                tile = tile * mask
            flat_ref[pl.ds(j, 16, stride=32), :] = tile
        for slot, pair in enumerate(PAIR_OF_SLOT):
            sent_ref[slot, first : first + 32, :] = flat_ref[pair * 32 : pair * 32 + 32, :].astype(BF16)


def _block_kernel(got_ref, first_ref, sent_ref, kept_ref):

    def block(offset):
        tall = []
        for zc in range(4):
            wide = []
            for zh in range(4):
                part = got_ref[zh * 4 + zc, offset : offset + 32, :]
                wide.append(jnp.concatenate([part[:, :64], part[:, 64:]], axis=0))
            tall.append(jnp.concatenate(wide, axis=1))
        return jnp.concatenate(tall, axis=0)

    amp = _perm(_perm(first_ref[0], block(0)), first_ref[1])
    src = block(32)
    kept_ref[...] = _perm(first_ref[0], src)
    swap = _perm(_perm(first_ref[2], src), first_ref[3])
    for x in range(4):
        for y in range(4):
            to = x * 4 + y
            sent_ref[to, :256, :] = amp[:, :128]
            sent_ref[to, 256:512, :] = amp[:, 128:]
            piece = swap[y * 64 : y * 64 + 64, x * 64 : x * 64 + 64]
            sent_ref[to, 512:, :] = jnp.concatenate([piece[:32], piece[32:]], axis=1)


def _ladder_kernel(
    place_ref, fac_ref, own_ref, other_ref, rows_ref, nat_ref, out_ref, sym_ref, inner_ref, left_ref, right_ref
):
    diagonal = place_ref[1] >= N_OFF
    for zh in range(4):
        part = _perm(rows_ref[...], fac_ref[zh * 256 : zh * 256 + 256, :])
        for y in range(4):
            right_ref[y * 256 + zh * 64 : y * 256 + zh * 64 + 64, :] = part[y * 64 : y * 64 + 64]
        for zc in range(4):
            for x in range(4):
                to = x * 256 + zc * 64 + zh * 16
                at = (zh * 4 + zc) * 64 + x * 16
                left_ref[to : to + 16, :] = fac_ref[at : at + 16, :]

    def gathered(ref, x, half):
        return [ref[x * 4 + y, half * 256 : half * 256 + 256, :] for y in range(4)]

    for i in range(4):
        for j in range(4):
            own = jnp.concatenate(gathered(own_ref, i, j // 2), axis=1)
            other = jnp.concatenate(gathered(other_ref, j, i // 2), axis=1)
            mine = jnp.concatenate(gathered(own_ref, j, i // 2), axis=1)
            other = jnp.where(diagonal, mine, other)
            total = lax.dot_general(own, nat_ref[j % 2], NT, preferred_element_type=F32)
            total += lax.dot_general(nat_ref[i % 2], other, NT, preferred_element_type=F32)
            sym_ref[i * 256 : i * 256 + 256, j * 256 : j * 256 + 256] = total.astype(BF16)
    for i in range(4):
        for j in range(4):
            inner_ref[i * 256 : i * 256 + 256, j * 256 : j * 256 + 256] = lax.dot_general(
                sym_ref[i * 256 : i * 256 + 256, :],
                right_ref[j * 256 : j * 256 + 256, :],
                NT,
                preferred_element_type=F32,
            ).astype(BF16)
    for x in range(4):
        for y in range(4):
            out_ref[x * 4 + y] = _perm(
                left_ref[x * 256 : x * 256 + 256, :], inner_ref[:, y * 256 : y * 256 + 256]
            )


def _sum_kernel(place_ref, part_ref, kept_ref, own_ref, other_ref, last_ref, sent_ref):
    diagonal = place_ref[1] >= N_OFF
    total = part_ref[0].astype(F32)
    for q in range(1, 16):
        total += part_ref[q].astype(F32)
    total += kept_ref[...].astype(F32)
    tall = []
    for x in range(4):
        wide = []
        for y in range(4):
            part = jnp.where(diagonal, own_ref[x * 4 + y], other_ref[x * 4 + y])
            wide.append(jnp.concatenate([part[:, :64], part[:, 64:]], axis=0))
        tall.append(jnp.concatenate(wide, axis=1))
    swap = jnp.concatenate(tall, axis=0)
    turned = lax.dot_general(last_ref[0], swap, NT, preferred_element_type=F32).astype(BF16)
    total += jnp.dot(turned, last_ref[1], preferred_element_type=F32)
    packed = _perm(last_ref[2], total.astype(BF16))
    for zh in range(4):
        for zc in range(4):
            piece = packed[zc * 64 : zc * 64 + 64, zh * 64 : zh * 64 + 64]
            sent_ref[zh * 4 + zc] = jnp.concatenate([piece[:32], piece[32:]], axis=1)


def _update_kernel(place_ref, occ_ref, rsym_ref, amps_ref, mask_ref, vir_ref, out_ref, flat_ref):
    row = place_ref[2]
    col = place_ref[3]
    exact = lax.Precision.HIGHEST

    def iota(shape, dim):
        return lax.broadcasted_iota(jnp.int32, shape, dim)

    mine = vir_ref[pl.ds(row // 2, 1), :]
    l_row = iota((32, 128), 1) - (row % 2) * 64
    in_row = (l_row // 2 == iota((32, 128), 0)) & (l_row >= 0)
    picked = jnp.where(in_row, jnp.broadcast_to(mine, (32, 128)), 0.0)
    same_half = (iota((128, 128), 0) % 2 == iota((128, 128), 1) // 64).astype(F32)
    vir_a = jnp.dot(picked, same_half, precision=exact, preferred_element_type=F32)
    lane = iota((128, 128), 1)
    want = ((lane // 4) % 2) * 64 + col * 4 + lane % 4
    choose = (iota((128, 128), 0) == want).astype(F32)
    by_block = jnp.dot(vir_ref[...], choose, precision=exact, preferred_element_type=F32)
    own_block = iota((8, 128), 0) == (iota((8, 128), 1) % 64) // 8
    vir_b = jnp.sum(jnp.where(own_block, by_block, 0.0), axis=0, keepdims=True)
    vir = vir_a + vir_b
    for slot, pair in enumerate(PAIR_OF_SLOT):
        denom = (occ_ref[pair // 4] + occ_ref[pair % 4]) - vir
        change = rsym_ref[slot].astype(F32) / denom
        old = amps_ref[slot].astype(F32)
        flat_ref[pair * 32 : pair * 32 + 32, :] = old + mask_ref[pair : pair + 1, :] * change
    for j in range(32):
        out_ref[:, j * 128 : (j + 1) * 128] = flat_ref[pl.ds(j, 16, stride=32), :].astype(BF16)


def _vmem(shape=None, index=None):
    if shape is None:
        return pl.BlockSpec(memory_space=pltpu.VMEM)
    return pl.BlockSpec(shape, index, memory_space=pltpu.VMEM)


SMEM = pl.BlockSpec(memory_space=pltpu.SMEM)


def _shards(tables, amps, source, factors, screen, occ_energy, vir_energy):
    first, last, rows_b, nat = tables
    x, zl, core = lax.axis_index("x"), lax.axis_index("zl"), lax.axis_index("core")
    zh, y = lax.axis_index("zh"), lax.axis_index("y")
    place = jnp.stack([x * 2 + zl, zh * 4 + zl * 2 + core, x * 4 + zl * 2 + core, zh * 4 + y])
    place = place.astype(jnp.int32)

    share = lax.all_to_all(factors, PLANE, 0, 0, tiled=True).reshape(64, 1024)
    fac = lax.all_gather(share, SLOTS, axis=0, tiled=True)

    sent, mask = pl.pallas_call(
        _mask_kernel,
        out_shape=(jax.ShapeDtypeStruct((16, 64, 128), BF16), jax.ShapeDtypeStruct((16, 128), F32)),
        in_specs=[SMEM, _vmem(), _vmem(), _vmem()],
        out_specs=(_vmem(), _vmem()),
        scratch_shapes=[pltpu.VMEM((512, 128), F32)],
        name="mask_amps",
    )(place, amps.reshape(16, 4096), source.reshape(16, 4096), screen.transpose(1, 0, 2))
    got = lax.all_to_all(sent, SLOTS, 0, 0, tiled=True)
    block, kept = pl.pallas_call(
        _block_kernel,
        out_shape=(jax.ShapeDtypeStruct((16, 544, 128), BF16), jax.ShapeDtypeStruct((256, 256), BF16)),
        in_specs=[_vmem(), _vmem()],
        out_specs=(_vmem(), _vmem()),
        compiler_params=VMEM,
        name="make_block",
    )(got, first)
    own = lax.all_to_all(block, PLANE, 0, 0, tiled=True)
    other = lax.ppermute(own, "core", [(0, 1), (1, 0)])
    square = pltpu.VMEM((1024, 1024), BF16)
    partial = pl.pallas_call(
        _ladder_kernel,
        out_shape=jax.ShapeDtypeStruct((16, 256, 256), BF16),
        in_specs=[SMEM] + [_vmem()] * 5,
        out_specs=_vmem(),
        scratch_shapes=[square] * 4,
        compiler_params=VMEM,
        name="ladder",
    )(place, fac, own, other, rows_b, nat)
    parts = lax.all_to_all(partial, PLANE, 0, 0, tiled=True)
    tail = _vmem((16, 32, 128), lambda i: (0, 16, 0))
    summed = pl.pallas_call(
        _sum_kernel,
        out_shape=jax.ShapeDtypeStruct((16, 32, 128), BF16),
        grid=(1,),
        in_specs=[SMEM, _vmem(), _vmem(), tail, tail, _vmem()],
        out_specs=_vmem(),
        compiler_params=VMEM,
        name="sum_parts",
    )(place, parts, kept, own, other, last)
    rsym = lax.all_to_all(summed, SLOTS, 0, 0, tiled=True)
    head = _vmem((16, 32, 128), lambda i: (0, 0, 0))
    out = pl.pallas_call(
        _update_kernel,
        out_shape=jax.ShapeDtypeStruct((16, 4096), BF16),
        grid=(1,),
        in_specs=[SMEM, SMEM, _vmem(), head, _vmem(), _vmem()],
        out_specs=_vmem(),
        scratch_shapes=[pltpu.VMEM((512, 128), F32)],
        name="update",
    )(place, occ_energy, rsym, sent, mask, vir_energy.reshape(8, 128))
    return out.reshape(1, 1, 16, 4096)


def solution(mesh):
    fine = Mesh(mesh.devices.reshape(4, 2, 2, 4, 4), AXES)
    row, col = ("x", "zl", "core"), ("zh", "y")
    in_specs = (
        P(row, col, None, None),
        P(row, col, None, None),
        P(None, row + col, None),
        P(),
        P(),
        P(),
    )
    shards = functools.partial(_shards, _tables())
    return jax.shard_map(shards, mesh=fine, in_specs=in_specs, out_specs=P(row, col, None, None), check_vma=False)
```

```python
import functools

import jax
import jax.numpy as jnp
import numpy as np
from jax import lax
from jax.experimental import pallas as pl
from jax.experimental.pallas import tpu as pltpu
from jax.sharding import Mesh
from jax.sharding import PartitionSpec as P

AXES = ("x", "zl", "core", "zh", "y")
PLANE = ("x", "y")
SLOTS = ("zh", "zl", "core")
DEEP = ("zl", "zh")
PAIR_OF_SLOT = (1, 4, 2, 8, 3, 12, 6, 9, 7, 13, 11, 14, 0, 5, 10, 15)
N_OFF = 12
VMEM = pltpu.CompilerParams(vmem_limit_bytes=40 * 1024 * 1024)
F32 = jnp.float32
BF16 = jnp.bfloat16
NT = (((1,), (1,)), ((), ()))
TN = (((0,), (0,)), ((), ()))


def _one_hot(source_of):
    source_of = np.asarray(source_of).reshape(-1)
    size = source_of.size
    out = np.zeros((size, size), np.float32)
    out[np.arange(size), source_of] = 1
    return out


def _grid(*sizes):
    return np.meshgrid(*[np.arange(s) for s in sizes], indexing="ij")


def _tables():
    zc, j, h = _grid(4, 32, 2)
    rows_nat = _one_hot(zc * 64 + h * 32 + j)
    rb, zh, k = _grid(16, 4, 4)
    cols_rb = _one_hot(zh * 64 + rb * 4 + k).T
    ya, zc, zh, k = _grid(4, 4, 4, 4)
    a_loc = zh * 16 + ya * 4 + k
    rows_src = _one_hot(zc * 64 + (a_loc % 2) * 32 + a_loc // 2)
    x, zh, zc, k = _grid(4, 4, 4, 4)
    cols_src = _one_hot(zh * 64 + (x * 4 + zc) * 4 + k).T
    first = np.stack([rows_nat, cols_rb, rows_src, cols_src])
    zc, zh, y, k = _grid(4, 4, 4, 4)
    swap_a = _one_hot(((y * 4 + zh) * 4 + zc) * 4 + k)
    zh, x, zc, k = _grid(4, 4, 4, 4)
    swap_b = _one_hot(((x * 4 + zc) * 4 + zh) * 4 + k).T
    last = np.stack([swap_a, swap_b, rows_nat.T])
    y, x, zc, k = _grid(4, 4, 4, 4)
    rows_b = _one_hot(((zc * 4 + x) * 4 + y) * 4 + k)
    nat = np.zeros((2, 256, 512), np.float32)
    for parity in range(2):
        y, rl, zh, k = _grid(4, 4, 4, 4)
        nat[parity, rl * 64 + zh * 16 + y * 4 + k, y * 128 + (parity * 4 + rl) * 16 + zh * 4 + k] = 1
    return [np.asarray(t, jnp.bfloat16) for t in (first, last, rows_b, nat)]


def _perm(left, right):
    return jnp.dot(left, right, preferred_element_type=F32).astype(BF16)


def _mask_kernel(place_ref, amps_ref, source_ref, screen_ref, sent_ref, mask_ref, flat_ref):
    block = screen_ref[place_ref[0]].astype(F32)
    lane_block = (lax.broadcasted_iota(jnp.int32, (8, 128), 1) % 64) // 8
    spread = (lax.broadcasted_iota(jnp.int32, (8, 128), 0) == lane_block).astype(F32)
    mask = lax.dot_general(block, spread, TN, preferred_element_type=F32)
    mask_ref[...] = mask
    for first, ref in ((0, amps_ref), (32, source_ref)):
        for j in range(32):
            tile = ref[:, j * 128 : (j + 1) * 128].astype(F32)
            if first == 0:
                tile = tile * mask
            flat_ref[pl.ds(j, 16, stride=32), :] = tile
        for slot, pair in enumerate(PAIR_OF_SLOT):
            sent_ref[slot, first : first + 32, :] = flat_ref[pair * 32 : pair * 32 + 32, :].astype(BF16)


def _block_kernel(got_ref, first_ref, sent_ref, kept_ref):

    def block(offset):
        tall = []
        for zc in range(4):
            wide = []
            for zh in range(4):
                part = got_ref[zh * 4 + zc, offset : offset + 32, :]
                wide.append(jnp.concatenate([part[:, :64], part[:, 64:]], axis=0))
            tall.append(jnp.concatenate(wide, axis=1))
        return jnp.concatenate(tall, axis=0)

    amp = _perm(_perm(first_ref[0], block(0)), first_ref[1])
    src = block(32)
    kept_ref[...] = _perm(first_ref[0], src)
    swap = _perm(_perm(first_ref[2], src), first_ref[3])
    for x in range(4):
        for y in range(4):
            to = x * 4 + y
            sent_ref[to, :256, :] = amp[:, :128]
            sent_ref[to, 256:512, :] = amp[:, 128:]
            piece = swap[y * 64 : y * 64 + 64, x * 64 : x * 64 + 64]
            sent_ref[to, 512:, :] = jnp.concatenate([piece[:32], piece[32:]], axis=1)


def _order_kernel(place_ref, *refs):
    deep = place_ref[1] // 2
    for k in range(8):
        refs[9][pl.ds(pl.multiple_of((deep + 8 - k) % 8 * 64, 64), 64), :] = refs[k][...]


def _ladder_kernel(
    place_ref,
    mine_ref,
    next_ref,
    own_ref,
    other_ref,
    rows_ref,
    nat_ref,
    out_ref,
    fac_ref,
    sym_ref,
    inner_ref,
    left_ref,
    right_ref,
):
    diagonal = place_ref[1] >= N_OFF
    core = place_ref[1] % 2
    for z in range(8):
        rows = slice(z * 64, z * 64 + 64)
        fac_ref[pl.ds(pl.multiple_of(z * 128 + core * 64, 64), 64), :] = mine_ref[rows, :]
        fac_ref[pl.ds(pl.multiple_of(z * 128 + 64 - core * 64, 64), 64), :] = next_ref[rows, :]
    for zh in range(4):
        part = _perm(rows_ref[...], fac_ref[zh * 256 : zh * 256 + 256, :])
        for y in range(4):
            right_ref[y * 256 + zh * 64 : y * 256 + zh * 64 + 64, :] = part[y * 64 : y * 64 + 64]
        for zc in range(4):
            for x in range(4):
                to = x * 256 + zc * 64 + zh * 16
                at = (zh * 4 + zc) * 64 + x * 16
                left_ref[to : to + 16, :] = fac_ref[at : at + 16, :]

    def gathered(ref, x, half):
        return [ref[x * 4 + y, half * 256 : half * 256 + 256, :] for y in range(4)]

    for i in range(4):
        for j in range(4):
            own = jnp.concatenate(gathered(own_ref, i, j // 2), axis=1)
            other = jnp.concatenate(gathered(other_ref, j, i // 2), axis=1)
            mine = jnp.concatenate(gathered(own_ref, j, i // 2), axis=1)
            other = jnp.where(diagonal, mine, other)
            total = lax.dot_general(own, nat_ref[j % 2], NT, preferred_element_type=F32)
            total += lax.dot_general(nat_ref[i % 2], other, NT, preferred_element_type=F32)
            sym_ref[i * 256 : i * 256 + 256, j * 256 : j * 256 + 256] = total.astype(BF16)
    for i in range(4):
        for j in range(4):
            inner_ref[i * 256 : i * 256 + 256, j * 256 : j * 256 + 256] = lax.dot_general(
                sym_ref[i * 256 : i * 256 + 256, :],
                right_ref[j * 256 : j * 256 + 256, :],
                NT,
                preferred_element_type=F32,
            ).astype(BF16)
    for x in range(4):
        for y in range(4):
            out_ref[x * 4 + y] = _perm(
                left_ref[x * 256 : x * 256 + 256, :], inner_ref[:, y * 256 : y * 256 + 256]
            )


def _sum_kernel(place_ref, part_ref, kept_ref, own_ref, other_ref, last_ref, sent_ref):
    diagonal = place_ref[1] >= N_OFF
    total = part_ref[0].astype(F32)
    for q in range(1, 16):
        total += part_ref[q].astype(F32)
    total += kept_ref[...].astype(F32)
    tall = []
    for x in range(4):
        wide = []
        for y in range(4):
            part = jnp.where(diagonal, own_ref[x * 4 + y], other_ref[x * 4 + y])
            wide.append(jnp.concatenate([part[:, :64], part[:, 64:]], axis=0))
        tall.append(jnp.concatenate(wide, axis=1))
    swap = jnp.concatenate(tall, axis=0)
    turned = lax.dot_general(last_ref[0], swap, NT, preferred_element_type=F32).astype(BF16)
    total += jnp.dot(turned, last_ref[1], preferred_element_type=F32)
    packed = _perm(last_ref[2], total.astype(BF16))
    for zh in range(4):
        for zc in range(4):
            piece = packed[zc * 64 : zc * 64 + 64, zh * 64 : zh * 64 + 64]
            sent_ref[zh * 4 + zc] = jnp.concatenate([piece[:32], piece[32:]], axis=1)


def _update_kernel(place_ref, occ_ref, rsym_ref, amps_ref, mask_ref, vir_ref, out_ref, flat_ref):
    row = place_ref[2]
    col = place_ref[3]
    exact = lax.Precision.HIGHEST

    def iota(shape, dim):
        return lax.broadcasted_iota(jnp.int32, shape, dim)

    mine = vir_ref[pl.ds(row // 2, 1), :]
    l_row = iota((32, 128), 1) - (row % 2) * 64
    in_row = (l_row // 2 == iota((32, 128), 0)) & (l_row >= 0)
    picked = jnp.where(in_row, jnp.broadcast_to(mine, (32, 128)), 0.0)
    same_half = (iota((128, 128), 0) % 2 == iota((128, 128), 1) // 64).astype(F32)
    vir_a = jnp.dot(picked, same_half, precision=exact, preferred_element_type=F32)
    lane = iota((128, 128), 1)
    want = ((lane // 4) % 2) * 64 + col * 4 + lane % 4
    choose = (iota((128, 128), 0) == want).astype(F32)
    by_block = jnp.dot(vir_ref[...], choose, precision=exact, preferred_element_type=F32)
    own_block = iota((8, 128), 0) == (iota((8, 128), 1) % 64) // 8
    vir_b = jnp.sum(jnp.where(own_block, by_block, 0.0), axis=0, keepdims=True)
    vir = vir_a + vir_b
    for slot, pair in enumerate(PAIR_OF_SLOT):
        denom = (occ_ref[pair // 4] + occ_ref[pair % 4]) - vir
        change = rsym_ref[slot].astype(F32) / denom
        old = amps_ref[slot].astype(F32)
        flat_ref[pair * 32 : pair * 32 + 32, :] = old + mask_ref[pair : pair + 1, :] * change
    for j in range(32):
        out_ref[:, j * 128 : (j + 1) * 128] = flat_ref[pl.ds(j, 16, stride=32), :].astype(BF16)


def _along_z(step):
    place = [(z % 2) * 4 + z // 2 for z in range(8)]
    return [(place[z], place[(z + step) % 8]) for z in range(8)]


def _vmem(shape=None, index=None):
    if shape is None:
        return pl.BlockSpec(memory_space=pltpu.VMEM)
    return pl.BlockSpec(shape, index, memory_space=pltpu.VMEM)


SMEM = pl.BlockSpec(memory_space=pltpu.SMEM)


def _shards(tables, amps, source, factors, screen, occ_energy, vir_energy):
    first, last, rows_b, nat = tables
    x, zl, core = lax.axis_index("x"), lax.axis_index("zl"), lax.axis_index("core")
    zh, y = lax.axis_index("zh"), lax.axis_index("y")
    place = jnp.stack([x * 2 + zl, zh * 4 + zl * 2 + core, x * 4 + zl * 2 + core, zh * 4 + y])
    place = place.astype(jnp.int32)

    share = lax.all_to_all(factors, PLANE, 0, 0, tiled=True).reshape(64, 1024)
    sent, mask = pl.pallas_call(
        _mask_kernel,
        out_shape=(jax.ShapeDtypeStruct((16, 64, 128), BF16), jax.ShapeDtypeStruct((16, 128), F32)),
        in_specs=[SMEM, _vmem(), _vmem(), _vmem()],
        out_specs=(_vmem(), _vmem()),
        scratch_shapes=[pltpu.VMEM((512, 128), F32)],
        name="mask_amps",
    )(place, amps.reshape(16, 4096), source.reshape(16, 4096), screen.transpose(1, 2, 0))
    share, sent = lax.optimization_barrier((share, sent))
    got = lax.all_to_all(sent, SLOTS, 0, 0, tiled=True)
    block, kept = pl.pallas_call(
        _block_kernel,
        out_shape=(jax.ShapeDtypeStruct((16, 544, 128), BF16), jax.ShapeDtypeStruct((256, 256), BF16)),
        in_specs=[_vmem(), _vmem()],
        out_specs=(_vmem(), _vmem()),
        compiler_params=VMEM,
        name="make_block",
    )(got, first)
    share, block = lax.optimization_barrier((share, block))
    pieces = [share] + [lax.ppermute(share, DEEP, _along_z(k)) for k in range(1, 8)]
    own = lax.all_to_all(block, PLANE, 0, 0, tiled=True)
    fac, own = pl.pallas_call(
        _order_kernel,
        out_shape=(jax.ShapeDtypeStruct((512, 1024), BF16), jax.ShapeDtypeStruct((16, 544, 128), BF16)),
        in_specs=[SMEM] + [_vmem()] * 8 + [pl.BlockSpec(memory_space=pl.ANY)],
        out_specs=(_vmem(), pl.BlockSpec(memory_space=pl.ANY)),
        input_output_aliases={9: 1},
        compiler_params=VMEM,
        name="order_factors",
    )(place, *pieces, own)
    other = lax.ppermute(own, "core", [(0, 1), (1, 0)])
    fac_other = lax.ppermute(fac, "core", [(0, 1), (1, 0)])
    square = pltpu.VMEM((1024, 1024), BF16)
    partial = pl.pallas_call(
        _ladder_kernel,
        out_shape=jax.ShapeDtypeStruct((16, 256, 256), BF16),
        in_specs=[SMEM] + [_vmem()] * 6,
        out_specs=_vmem(),
        scratch_shapes=[square] * 5,
        compiler_params=VMEM,
        name="ladder",
    )(place, fac, fac_other, own, other, rows_b, nat)
    parts = lax.all_to_all(partial, PLANE, 0, 0, tiled=True)
    tail = _vmem((16, 32, 128), lambda i: (0, 16, 0))
    summed = pl.pallas_call(
        _sum_kernel,
        out_shape=jax.ShapeDtypeStruct((16, 32, 128), BF16),
        grid=(1,),
        in_specs=[SMEM, _vmem(), _vmem(), tail, tail, _vmem()],
        out_specs=_vmem(),
        compiler_params=VMEM,
        name="sum_parts",
    )(place, parts, kept, own, other, last)
    rsym = lax.all_to_all(summed, SLOTS, 0, 0, tiled=True)
    head = _vmem((16, 32, 128), lambda i: (0, 0, 0))
    out = pl.pallas_call(
        _update_kernel,
        out_shape=jax.ShapeDtypeStruct((16, 4096), BF16),
        grid=(1,),
        in_specs=[SMEM, SMEM, _vmem(), head, _vmem(), _vmem()],
        out_specs=_vmem(),
        scratch_shapes=[pltpu.VMEM((512, 128), F32)],
        name="update",
    )(place, occ_energy, rsym, sent, mask, vir_energy.reshape(8, 128))
    return out.reshape(1, 1, 16, 4096)


def solution(mesh):
    fine = Mesh(mesh.devices.reshape(4, 2, 2, 4, 4), AXES)
    row, col = ("x", "zl", "core"), ("zh", "y")
    in_specs = (
        P(row, col, None, None),
        P(row, col, None, None),
        P(None, row + col, None),
        P(),
        P(),
        P(),
    )
    shards = functools.partial(_shards, _tables())
    return jax.shard_map(shards, mesh=fine, in_specs=in_specs, out_specs=P(row, col, None, None), check_vma=False)
```

```python
import functools

import jax
import jax.numpy as jnp
import numpy as np
from jax import lax
from jax.experimental import pallas as pl
from jax.experimental.pallas import tpu as pltpu
from jax.sharding import Mesh
from jax.sharding import PartitionSpec as P

AXES = ("x", "zl", "core", "zh", "y")
ROWS = ("x", "zl", "core")
COLS = ("zh", "y")
CHIPS = ("x", "zl")
VMEM = pltpu.CompilerParams(vmem_limit_bytes=40 * 1024 * 1024)
F32 = jnp.float32
BF16 = jnp.bfloat16
NT = (((1,), (1,)), ((), ()))
TN = (((0,), (0,)), ((), ()))


def _one_hot(source_of):
    source_of = np.asarray(source_of).reshape(-1)
    size = source_of.size
    out = np.zeros((size, size), np.float32)
    out[np.arange(size), source_of] = 1
    return out


def _grid(*sizes):
    return np.meshgrid(*[np.arange(s) for s in sizes], indexing="ij")


def _tables():
    j, h = _grid(32, 2)
    rows = _one_hot(h * 32 + j)
    small = np.stack([rows, rows.T, np.eye(64, dtype=np.float32)])
    row, col, k = _grid(16, 16, 4)
    wide = _one_hot(col * 64 + row * 4 + k).T
    row, col, k = _grid(4, 16, 4)
    rows_b = _one_hot(col * 16 + row * 4 + k)
    return [np.asarray(t, jnp.bfloat16) for t in (small, wide, rows_b)]


def _perm(left, right):
    return jnp.dot(left, right, preferred_element_type=F32).astype(BF16)


def _unpack(part):
    return jnp.concatenate([part[:, :64], part[:, 64:]], axis=0)


def _pack(piece):
    return jnp.concatenate([piece[:32], piece[32:]], axis=1)


def _spread_kernel(fac_ref, out_ref, sems):
    copies = [pltpu.make_async_copy(fac_ref, out_ref.at[k * 16 : k * 16 + 16], sems.at[k]) for k in range(4)]
    for copy in copies:
        copy.start()
    for copy in copies:
        copy.wait()


def _mask_kernel(place_ref, amps_ref, source_ref, screen_ref, sent_ref, mask_ref, flat_ref):
    block = screen_ref[place_ref[0]].astype(F32)
    lane_block = (lax.broadcasted_iota(jnp.int32, (8, 128), 1) % 64) // 8
    spread = (lax.broadcasted_iota(jnp.int32, (8, 128), 0) == lane_block).astype(F32)
    mask = lax.dot_general(block, spread, TN, preferred_element_type=F32)
    mask_ref[...] = mask
    for first, ref in ((0, amps_ref), (32, source_ref)):
        for j in range(32):
            tile = ref[:, j * 128 : (j + 1) * 128].astype(F32)
            if first == 0:
                tile = tile * mask
            flat_ref[pl.ds(j, 16, stride=32), :] = tile
        for pair in range(16):
            sent_ref[pair, first : first + 32, :] = flat_ref[pair * 32 : pair * 32 + 32, :].astype(BF16)


def _block_kernel(got_ref, small_ref, wide_ref, near_ref, far_ref, sent_ref, kept_ref, amp_ref, src_ref, sems):
    del near_ref, far_ref

    def block(offset):
        wide = jnp.concatenate([_unpack(got_ref[c, offset : offset + 32, :]) for c in range(16)], axis=1)
        return _perm(small_ref[0], wide)

    amp_ref[...] = _perm(block(0), wide_ref[...])
    copies = [pltpu.make_async_copy(amp_ref, sent_ref.at[to], sems.at[to]) for to in range(8)]
    for copy in copies:
        copy.start()
    src_ref[...] = block(32)
    copies.append(pltpu.make_async_copy(src_ref, kept_ref, sems.at[8]))
    copies[8].start()
    for copy in copies:
        copy.wait()


def _gate_kernel(own_ref, last_ref, out_ref):
    del own_ref, last_ref, out_ref


def _ladder_kernel(
    place_ref,
    mine_ref,
    near_ref,
    far_ref,
    last_ref,
    own_ref,
    other_ref,
    rows_ref,
    keep_ref,
    give_ref,
    amp_ref,
    inner_ref,
    left_ref,
    right_ref,
    sems,
):
    core, y = place_ref[1], place_ref[3]
    behind, ahead, across = (y + 3) % 4, (y + 1) % 4, (y + 2) % 4
    copies = (
        pltpu.make_async_copy(mine_ref, right_ref.at[:, y], sems.at[0]),
        pltpu.make_async_copy(near_ref, right_ref.at[:, behind], sems.at[1]),
        pltpu.make_async_copy(far_ref, right_ref.at[:, ahead], sems.at[2]),
        pltpu.make_async_copy(last_ref, right_ref.at[:, across], sems.at[3]),
        pltpu.make_async_copy(own_ref, amp_ref.at[:, core], sems.at[4]),
        pltpu.make_async_copy(other_ref, amp_ref.at[:, 1 - core], sems.at[5]),
    )
    for copy in copies:
        copy.start()
    for copy in copies[:4]:
        copy.wait()
    for x in range(4):
        rows = [right_ref[col // 4, col % 4, x * 16 : x * 16 + 16, :] for col in range(16)]
        left_ref[x * 256 : x * 256 + 256, :] = _perm(rows_ref[...], jnp.concatenate(rows, axis=0))
    for copy in copies[4:]:
        copy.wait()
    for i in range(4):
        for j in range(4):
            inner_ref[i * 256 : i * 256 + 256, j * 256 : j * 256 + 256] = lax.dot_general(
                amp_ref[i * 2 : i * 2 + 2].reshape(256, 1024),
                right_ref[j].reshape(256, 1024),
                NT,
                preferred_element_type=F32,
            ).astype(BF16)
    first = core == 0
    for x in range(4):
        for j in range(4):
            cols = slice(j * 256, j * 256 + 256)
            part = _perm(left_ref[x * 256 : x * 256 + 256, :], inner_ref[:, cols])
            for zl in range(2):
                zero = part[zl * 128 : zl * 128 + 64]
                one = part[zl * 128 + 64 : zl * 128 + 128]
                keep_ref[x * 2 + zl, :, cols] = jnp.where(first, zero, one)
                give_ref[x * 2 + zl, :, cols] = jnp.where(first, one, zero)


def _sum_kernel(part_ref, kept_ref, wide_ref, resid_ref, sent_ref):
    total = kept_ref[...].astype(F32)
    for chip in range(8):
        total += part_ref[chip].astype(F32)
    resid = total.astype(BF16)
    resid_ref[...] = resid
    natural = _perm(resid, wide_ref[...])
    for row in range(16):
        sent_ref[row] = _pack(natural[:, row * 64 : row * 64 + 64])


def _swap_kernel(got_ref, resid_ref, small_ref, wide_ref, sent_ref):
    tall = jnp.concatenate([_unpack(got_ref[row]) for row in range(16)], axis=0)
    turned = lax.dot_general(small_ref[2], tall, NT, preferred_element_type=F32).astype(BF16)
    turned = lax.dot_general(turned, wide_ref[...], NT, preferred_element_type=F32).astype(BF16)
    straight = _perm(small_ref[1], resid_ref[...])
    turned = _perm(small_ref[1], turned)
    for col in range(16):
        sent_ref[col, :32, :] = _pack(straight[:, col * 64 : col * 64 + 64])
        sent_ref[col, 32:, :] = _pack(turned[:, col * 64 : col * 64 + 64])


def _update_kernel(place_ref, occ_ref, resid_ref, amps_ref, mask_ref, vir_ref, out_ref, flat_ref):
    row = place_ref[5]
    col = place_ref[4]
    exact = lax.Precision.HIGHEST

    def iota(shape, dim):
        return lax.broadcasted_iota(jnp.int32, shape, dim)

    mine = vir_ref[pl.ds(row // 2, 1), :]
    l_row = iota((32, 128), 1) - (row % 2) * 64
    in_row = (l_row // 2 == iota((32, 128), 0)) & (l_row >= 0)
    picked = jnp.where(in_row, jnp.broadcast_to(mine, (32, 128)), 0.0)
    same_half = (iota((128, 128), 0) % 2 == iota((128, 128), 1) // 64).astype(F32)
    vir_a = jnp.dot(picked, same_half, precision=exact, preferred_element_type=F32)
    lane = iota((128, 128), 1)
    want = ((lane // 4) % 2) * 64 + col * 4 + lane % 4
    choose = (iota((128, 128), 0) == want).astype(F32)
    by_block = jnp.dot(vir_ref[...], choose, precision=exact, preferred_element_type=F32)
    own_block = iota((8, 128), 0) == (iota((8, 128), 1) % 64) // 8
    vir_b = jnp.sum(jnp.where(own_block, by_block, 0.0), axis=0, keepdims=True)
    vir = vir_a + vir_b
    for pair in range(16):
        i, j = pair // 4, pair % 4
        denom = (occ_ref[i] + occ_ref[j]) - vir
        rsym = resid_ref[pair, :32].astype(F32) + resid_ref[j * 4 + i, 32:].astype(F32)
        old = amps_ref[pair].astype(F32)
        flat_ref[pair * 32 : pair * 32 + 32, :] = old + mask_ref[pair : pair + 1, :] * (rsym / denom)
    for j in range(32):
        out_ref[:, j * 128 : (j + 1) * 128] = flat_ref[pl.ds(j, 16, stride=32), :].astype(BF16)


def _vmem(shape=None, index=None):
    if shape is None:
        return pl.BlockSpec(memory_space=pltpu.VMEM)
    return pl.BlockSpec(shape, index, memory_space=pltpu.VMEM)


SMEM = pl.BlockSpec(memory_space=pltpu.SMEM)
HBM = pl.BlockSpec(memory_space=pltpu.HBM)


def _sds(*shape, dtype=BF16):
    return jax.ShapeDtypeStruct(shape, dtype)


def _turn(value, step):
    return lax.ppermute(value, "y", [(i, (i + step) % 4) for i in range(4)])


def _shards(tables, amps, source, factors, screen, occ_energy, vir_energy):
    small, wide, rows_b = tables
    x, zl, core = lax.axis_index("x"), lax.axis_index("zl"), lax.axis_index("core")
    zh, y = lax.axis_index("zh"), lax.axis_index("y")
    place = jnp.stack([x * 2 + zl, core, zh, y, zh * 4 + y, x * 4 + zl * 2 + core]).astype(jnp.int32)

    spread = pl.pallas_call(
        _spread_kernel,
        out_shape=_sds(64, 4, 1024),
        in_specs=[_vmem()],
        out_specs=HBM,
        scratch_shapes=[pltpu.SemaphoreType.DMA((4,))],
        name="spread_factors",
    )(factors)
    fac = lax.all_to_all(spread, ("zh",) + ROWS, 0, 0, tiled=True).reshape(4, 64, 1024)
    sent, mask = pl.pallas_call(
        _mask_kernel,
        out_shape=(_sds(16, 64, 128), _sds(16, 128, dtype=F32)),
        in_specs=[SMEM, _vmem(), _vmem(), _vmem()],
        out_specs=(_vmem(), _vmem()),
        scratch_shapes=[pltpu.VMEM((512, 128), F32)],
        name="mask_amps",
    )(place, amps.reshape(16, 4096), source.reshape(16, 4096), screen.transpose(1, 2, 0))
    fac, sent = lax.optimization_barrier((fac, sent))
    near, far = _turn(fac, 1), _turn(fac, 3)
    opposite = _turn(near, 1)
    got = lax.all_to_all(sent, COLS, 0, 0, tiled=True)
    block, kept = pl.pallas_call(
        _block_kernel,
        out_shape=(_sds(8, 64, 1024), _sds(64, 1024)),
        in_specs=[_vmem(), _vmem(), _vmem(), HBM, HBM],
        out_specs=(HBM, HBM),
        scratch_shapes=[
            pltpu.VMEM((64, 1024), BF16),
            pltpu.VMEM((64, 1024), BF16),
            pltpu.SemaphoreType.DMA((9,)),
        ],
        compiler_params=VMEM,
        name="make_block",
    )(got, small, wide, near, far)
    own = lax.all_to_all(block, CHIPS, 0, 0, tiled=True)
    own = pl.pallas_call(
        _gate_kernel,
        out_shape=_sds(8, 64, 1024),
        in_specs=[HBM] * 2,
        out_specs=HBM,
        input_output_aliases={0: 0},
        compiler_params=VMEM,
        name="gate",
    )(own, opposite)
    other = lax.ppermute(own, "core", [(0, 1), (1, 0)])
    square = pltpu.VMEM((1024, 1024), BF16)
    keep, give = pl.pallas_call(
        _ladder_kernel,
        out_shape=(_sds(8, 64, 1024), _sds(8, 64, 1024)),
        in_specs=[SMEM] + [HBM] * 6 + [_vmem()],
        out_specs=(_vmem(), _vmem()),
        scratch_shapes=[
            pltpu.VMEM((8, 2, 64, 1024), BF16),
            square,
            square,
            pltpu.VMEM((4, 4, 64, 1024), BF16),
            pltpu.SemaphoreType.DMA((6,)),
        ],
        compiler_params=VMEM,
        name="ladder",
    )(place, fac, near, far, opposite, own, other, rows_b)
    taken = lax.ppermute(give, "core", [(0, 1), (1, 0)])
    partial = (keep.astype(F32) + taken.astype(F32)).astype(BF16)
    parts = lax.all_to_all(partial, CHIPS, 0, 0, tiled=True)
    resid, turn = pl.pallas_call(
        _sum_kernel,
        out_shape=(_sds(64, 1024), _sds(16, 32, 128)),
        in_specs=[_vmem()] * 3,
        out_specs=(_vmem(), _vmem()),
        compiler_params=VMEM,
        name="sum_parts",
    )(parts, kept, wide)
    turned = lax.all_to_all(turn, ROWS, 0, 0, tiled=True)
    last = pl.pallas_call(
        _swap_kernel,
        out_shape=_sds(16, 64, 128),
        in_specs=[_vmem()] * 4,
        out_specs=_vmem(),
        compiler_params=VMEM,
        name="swap_virtuals",
    )(turned, resid, small, wide)
    back = lax.all_to_all(last, COLS, 0, 0, tiled=True)
    head = _vmem((16, 32, 128), lambda i: (0, 0, 0))
    out = pl.pallas_call(
        _update_kernel,
        out_shape=_sds(16, 4096),
        grid=(1,),
        in_specs=[SMEM, SMEM, _vmem(), head, _vmem(), _vmem()],
        out_specs=_vmem(),
        scratch_shapes=[pltpu.VMEM((512, 128), F32)],
        name="update",
    )(place, occ_energy, back, sent, mask, vir_energy.reshape(8, 128))
    return out.reshape(1, 1, 16, 4096)


def solution(mesh):
    fine = Mesh(mesh.devices.reshape(4, 2, 2, 4, 4), AXES)
    in_specs = (
        P(ROWS, COLS, None, None),
        P(ROWS, COLS, None, None),
        P(None, ROWS + COLS, None),
        P(),
        P(),
        P(),
    )
    shards = functools.partial(_shards, _tables())
    return jax.shard_map(shards, mesh=fine, in_specs=in_specs, out_specs=P(ROWS, COLS, None, None), check_vma=False)
```

```python
import functools

import jax
import jax.numpy as jnp
import numpy as np
from jax import lax
from jax.experimental import pallas as pl
from jax.experimental.pallas import tpu as pltpu
from jax.sharding import Mesh
from jax.sharding import PartitionSpec as P

AXES = ("x", "zl", "core", "zh", "y")
ROWS = ("x", "zl", "core")
COLS = ("zh", "y")
CHIPS = ("x", "zl")
VMEM = pltpu.CompilerParams(vmem_limit_bytes=40 * 1024 * 1024)
F32 = jnp.float32
BF16 = jnp.bfloat16
NT = (((1,), (1,)), ((), ()))
TN = (((0,), (0,)), ((), ()))


def _one_hot(source_of):
    source_of = np.asarray(source_of).reshape(-1)
    size = source_of.size
    out = np.zeros((size, size), np.float32)
    out[np.arange(size), source_of] = 1
    return out


def _grid(*sizes):
    return np.meshgrid(*[np.arange(s) for s in sizes], indexing="ij")


def _tables():
    j, h = _grid(32, 2)
    rows = _one_hot(h * 32 + j)
    small = np.stack([rows, rows.T, np.eye(64, dtype=np.float32)])
    row, col, k = _grid(16, 16, 4)
    wide = _one_hot(col * 64 + row * 4 + k).T
    row, col, k = _grid(4, 16, 4)
    rows_b = _one_hot(col * 16 + row * 4 + k)
    return [np.asarray(t, jnp.bfloat16) for t in (small, wide, rows_b)]


def _perm(left, right):
    return jnp.dot(left, right, preferred_element_type=F32).astype(BF16)


def _unpack(part):
    return jnp.concatenate([part[:, :64], part[:, 64:]], axis=0)


def _pack(piece):
    return jnp.concatenate([piece[:32], piece[32:]], axis=1)


def _spread_kernel(fac_ref, out_ref, sems):
    copies = [pltpu.make_async_copy(fac_ref, out_ref.at[k * 16 : k * 16 + 16], sems.at[k]) for k in range(4)]
    for copy in copies:
        copy.start()
    for copy in copies:
        copy.wait()


def _mask_kernel(
    place_ref,
    amps_ref,
    source_ref,
    screen_ref,
    held_ref,
    mask_ref,
    out0,
    out1,
    out2,
    out3,
    flat_ref,
    flat2_ref,
):
    block = screen_ref[place_ref[0]].astype(F32)
    lane_block = (lax.broadcasted_iota(jnp.int32, (8, 128), 1) % 64) // 8
    spread = (lax.broadcasted_iota(jnp.int32, (8, 128), 0) == lane_block).astype(F32)
    mask = lax.dot_general(block, spread, TN, preferred_element_type=F32)
    mask_ref[...] = mask
    y = place_ref[3]
    for j in range(32):
        tile = slice(j * 128, (j + 1) * 128)
        flat_ref[pl.ds(j, 16, stride=32), :] = amps_ref[:, tile].astype(F32) * mask
        flat2_ref[pl.ds(j, 16, stride=32), :] = source_ref[:, tile].astype(F32)
    for pair in range(16):
        held_ref[pair, :32] = flat_ref[pair * 32 : pair * 32 + 32, :].astype(BF16)
        held_ref[pair, 32:] = flat2_ref[pair * 32 : pair * 32 + 32, :].astype(BF16)
    for k, out in enumerate((out0, out1, out2, out3)):
        to = (y + k) % 4
        for zh in range(4):
            rows = pl.ds(pl.multiple_of(zh * 128 + to * 32, 32), 32)
            turned = pl.ds(pl.multiple_of(to * 128 + zh * 32, 32), 32)
            out[zh, :32, :] = flat_ref[rows, :].astype(BF16)
            out[zh, 32:64, :] = flat_ref[turned, :].astype(BF16)
            out[zh, 64:, :] = flat2_ref[turned, :].astype(BF16)


def _relay_kernel(place_ref, in0, in1, in2, in3, out0, out1, out2, out3):
    zh, y = place_ref[2], place_ref[3]
    for m, out in enumerate((out0, out1, out2, out3)):
        for k, ref in enumerate((in0, in1, in2, in3)):
            out[(y + 4 - k) % 4] = ref[(zh + m) % 4]


def _block_kernel(place_ref, in0, in1, in2, in3, small_ref, wide_ref, amp_ref, sent_ref, got_ref):
    zh = place_ref[2]
    for m, ref in enumerate((in0, in1, in2, in3)):
        got_ref[(zh + 4 - m) % 4] = ref[...]

    def block(offset):
        parts = [_unpack(got_ref[c // 4, c % 4, offset : offset + 32, :]) for c in range(16)]
        return _perm(small_ref[0], jnp.concatenate(parts, axis=1))

    whole = jnp.concatenate([block(0), block(32), block(64)], axis=0)
    whole = _perm(whole, wide_ref[...])
    amp_ref[...] = whole[:64]
    for row in range(16):
        cols = slice(row * 64, row * 64 + 64)
        sent_ref[row, :32, :] = _pack(whole[64:128, cols])
        sent_ref[row, 32:, :] = _pack(whole[128:, cols])


def _symmetric_kernel(
    got_ref, amp_ref, small_ref, wide_ref, near_ref, far_ref, last_ref, sent_ref, kept_ref
):
    del near_ref, far_ref, last_ref

    def turned(offset):
        tall = jnp.concatenate([_unpack(got_ref[row, offset : offset + 32, :]) for row in range(16)], axis=0)
        return lax.dot_general(small_ref[2], tall, NT, preferred_element_type=F32)

    block = (amp_ref[...].astype(F32) + turned(0)).astype(BF16)
    for to in range(8):
        sent_ref[to] = block
    source = turned(32).astype(BF16)
    kept_ref[...] = lax.dot_general(source, wide_ref[...], NT, preferred_element_type=F32).astype(BF16)


def _gate_kernel(value_ref, small_ref, out_ref):
    del value_ref, small_ref, out_ref


def _ladder_kernel(
    place_ref,
    mine_ref,
    near_ref,
    far_ref,
    last_ref,
    own_ref,
    other_ref,
    rows_ref,
    keep_ref,
    give_ref,
    amp_ref,
    inner_ref,
    left_ref,
    right_ref,
    sems,
):
    core, y = place_ref[1], place_ref[3]
    behind, ahead, across = (y + 3) % 4, (y + 1) % 4, (y + 2) % 4
    copies = (
        pltpu.make_async_copy(mine_ref, right_ref.at[:, y], sems.at[0]),
        pltpu.make_async_copy(near_ref, right_ref.at[:, behind], sems.at[1]),
        pltpu.make_async_copy(far_ref, right_ref.at[:, ahead], sems.at[2]),
        pltpu.make_async_copy(last_ref, right_ref.at[:, across], sems.at[3]),
        pltpu.make_async_copy(own_ref, amp_ref.at[:, core], sems.at[4]),
        pltpu.make_async_copy(other_ref, amp_ref.at[:, 1 - core], sems.at[5]),
    )
    for copy in copies:
        copy.start()
    for copy in copies[:4]:
        copy.wait()
    for x in range(4):
        rows = [right_ref[col // 4, col % 4, x * 16 : x * 16 + 16, :] for col in range(16)]
        left_ref[x * 256 : x * 256 + 256, :] = _perm(rows_ref[...], jnp.concatenate(rows, axis=0))
    for copy in copies[4:]:
        copy.wait()
    for i in range(4):
        for j in range(4):
            inner_ref[i * 256 : i * 256 + 256, j * 256 : j * 256 + 256] = lax.dot_general(
                amp_ref[i * 2 : i * 2 + 2].reshape(256, 1024),
                right_ref[j].reshape(256, 1024),
                NT,
                preferred_element_type=F32,
            ).astype(BF16)
    first = core == 0
    for x in range(4):
        for j in range(4):
            cols = slice(j * 256, j * 256 + 256)
            part = _perm(left_ref[x * 256 : x * 256 + 256, :], inner_ref[:, cols])
            for zl in range(2):
                zero = part[zl * 128 : zl * 128 + 64]
                one = part[zl * 128 + 64 : zl * 128 + 128]
                keep_ref[x * 2 + zl, :, cols] = jnp.where(first, zero, one)
                give_ref[x * 2 + zl, :, cols] = jnp.where(first, one, zero)


def _sum_kernel(part_ref, kept_ref, small_ref, sent_ref):
    total = kept_ref[...].astype(F32)
    for chip in range(8):
        total += part_ref[chip].astype(F32)
    total = _perm(small_ref[1], total.astype(BF16))
    for col in range(16):
        sent_ref[col] = _pack(total[:, col * 64 : col * 64 + 64])


def _update_kernel(place_ref, occ_ref, resid_ref, held_ref, mask_ref, vir_ref, out_ref, flat_ref):
    row = place_ref[5]
    col = place_ref[4]
    exact = lax.Precision.HIGHEST

    def iota(shape, dim):
        return lax.broadcasted_iota(jnp.int32, shape, dim)

    mine = vir_ref[pl.ds(row // 2, 1), :]
    l_row = iota((32, 128), 1) - (row % 2) * 64
    in_row = (l_row // 2 == iota((32, 128), 0)) & (l_row >= 0)
    picked = jnp.where(in_row, jnp.broadcast_to(mine, (32, 128)), 0.0)
    same_half = (iota((128, 128), 0) % 2 == iota((128, 128), 1) // 64).astype(F32)
    vir_a = jnp.dot(picked, same_half, precision=exact, preferred_element_type=F32)
    lane = iota((128, 128), 1)
    want = ((lane // 4) % 2) * 64 + col * 4 + lane % 4
    choose = (iota((128, 128), 0) == want).astype(F32)
    by_block = jnp.dot(vir_ref[...], choose, precision=exact, preferred_element_type=F32)
    own_block = iota((8, 128), 0) == (iota((8, 128), 1) % 64) // 8
    vir_b = jnp.sum(jnp.where(own_block, by_block, 0.0), axis=0, keepdims=True)
    vir = vir_a + vir_b
    for pair in range(16):
        i, j = pair // 4, pair % 4
        denom = (occ_ref[i] + occ_ref[j]) - vir
        rsym = resid_ref[pair].astype(F32) + held_ref[pair, 32:].astype(F32)
        old = held_ref[pair, :32].astype(F32)
        flat_ref[pair * 32 : pair * 32 + 32, :] = old + mask_ref[pair : pair + 1, :] * (rsym / denom)
    for j in range(32):
        out_ref[:, j * 128 : (j + 1) * 128] = flat_ref[pl.ds(j, 16, stride=32), :].astype(BF16)


def _vmem():
    return pl.BlockSpec(memory_space=pltpu.VMEM)


SMEM = pl.BlockSpec(memory_space=pltpu.SMEM)
HBM = pl.BlockSpec(memory_space=pltpu.HBM)
ANY = pl.BlockSpec(memory_space=pl.ANY)


def _sds(*shape, dtype=BF16):
    return jax.ShapeDtypeStruct(shape, dtype)


def _turn(value, axis, step):
    if step == 0:
        return value
    return lax.ppermute(value, axis, [(i, (i + step) % 4) for i in range(4)])


def _swap_cores(value):
    return lax.ppermute(value, "core", [(0, 1), (1, 0)])


def _after(value, small):
    return pl.pallas_call(
        _gate_kernel,
        out_shape=jax.ShapeDtypeStruct(value.shape, value.dtype),
        in_specs=[ANY, ANY],
        out_specs=ANY,
        input_output_aliases={0: 0},
        name="gate",
    )(value, small)


def _shards(tables, amps, source, factors, screen, occ_energy, vir_energy):
    small, wide, rows_b = tables
    x, zl, core = lax.axis_index("x"), lax.axis_index("zl"), lax.axis_index("core")
    zh, y = lax.axis_index("zh"), lax.axis_index("y")
    place = jnp.stack([x * 2 + zl, core, zh, y, zh * 4 + y, x * 4 + zl * 2 + core]).astype(jnp.int32)

    spread = pl.pallas_call(
        _spread_kernel,
        out_shape=_sds(64, 4, 1024),
        in_specs=[_vmem()],
        out_specs=HBM,
        scratch_shapes=[pltpu.SemaphoreType.DMA((4,))],
        name="spread_factors",
    )(factors)
    fac = lax.all_to_all(spread, ("zh",) + ROWS, 0, 0, tiled=True).reshape(4, 64, 1024)
    four = _sds(4, 96, 128)
    held, mask, *outs = pl.pallas_call(
        _mask_kernel,
        out_shape=(_sds(16, 64, 128), _sds(16, 128, dtype=F32)) + (four,) * 4,
        in_specs=[SMEM, _vmem(), _vmem(), _vmem()],
        out_specs=(_vmem(),) * 6,
        scratch_shapes=[pltpu.VMEM((512, 128), F32)] * 2,
        name="mask_amps",
    )(place, amps.reshape(16, 4096), source.reshape(16, 4096), screen.transpose(1, 2, 0))
    outs = [_turn(out, "y", k) for k, out in enumerate(outs)]
    outs = pl.pallas_call(
        _relay_kernel,
        out_shape=(four,) * 4,
        in_specs=[SMEM] + [_vmem()] * 4,
        out_specs=(_vmem(),) * 4,
        name="relay",
    )(place, *outs)
    fac = _after(fac, outs[1])
    outs = [_turn(out, "zh", k) for k, out in enumerate(outs)]
    near, far = _turn(fac, "y", 1), _turn(fac, "y", 3)
    opposite = _turn(fac, "y", 2)
    block, turn = pl.pallas_call(
        _block_kernel,
        out_shape=(_sds(64, 1024), _sds(16, 64, 128)),
        in_specs=[SMEM] + [_vmem()] * 6,
        out_specs=(_vmem(), _vmem()),
        scratch_shapes=[pltpu.VMEM((4, 4, 96, 128), BF16)],
        compiler_params=VMEM,
        name="make_block",
    )(place, *outs, small, wide)
    turn = lax.all_to_all(turn, ROWS, 0, 0, tiled=True)
    block, kept = pl.pallas_call(
        _symmetric_kernel,
        out_shape=(_sds(8, 64, 1024), _sds(64, 1024)),
        in_specs=[_vmem()] * 4 + [ANY] * 3,
        out_specs=(_vmem(), _vmem()),
        compiler_params=VMEM,
        name="symmetrize",
    )(turn, block, small, wide, near, far, opposite)
    own = lax.all_to_all(block, CHIPS, 0, 0, tiled=True)
    other = _swap_cores(own)
    square = pltpu.VMEM((1024, 1024), BF16)
    keep, give = pl.pallas_call(
        _ladder_kernel,
        out_shape=(_sds(8, 64, 1024), _sds(8, 64, 1024)),
        in_specs=[SMEM] + [HBM] * 6 + [_vmem()],
        out_specs=(_vmem(), _vmem()),
        scratch_shapes=[
            pltpu.VMEM((8, 2, 64, 1024), BF16),
            square,
            square,
            pltpu.VMEM((4, 4, 64, 1024), BF16),
            pltpu.SemaphoreType.DMA((6,)),
        ],
        compiler_params=VMEM,
        name="ladder",
    )(place, fac, near, far, opposite, own, other, rows_b)
    taken = _swap_cores(give)
    partial = (keep.astype(F32) + taken.astype(F32)).astype(BF16)
    parts = lax.all_to_all(partial, CHIPS, 0, 0, tiled=True)
    last = pl.pallas_call(
        _sum_kernel,
        out_shape=_sds(16, 32, 128),
        in_specs=[_vmem()] * 3,
        out_specs=_vmem(),
        compiler_params=VMEM,
        name="sum_parts",
    )(parts, kept, small)
    back = lax.all_to_all(last, COLS, 0, 0, tiled=True)
    out = pl.pallas_call(
        _update_kernel,
        out_shape=_sds(16, 4096),
        in_specs=[SMEM, SMEM, _vmem(), _vmem(), _vmem(), _vmem()],
        out_specs=_vmem(),
        scratch_shapes=[pltpu.VMEM((512, 128), F32)],
        name="update",
    )(place, occ_energy, back, held, mask, vir_energy.reshape(8, 128))
    return out.reshape(1, 1, 16, 4096)


def solution(mesh):
    fine = Mesh(mesh.devices.reshape(4, 2, 2, 4, 4), AXES)
    in_specs = (
        P(ROWS, COLS, None, None),
        P(ROWS, COLS, None, None),
        P(None, ROWS + COLS, None),
        P(),
        P(),
        P(),
    )
    shards = functools.partial(_shards, _tables())
    return jax.shard_map(shards, mesh=fine, in_specs=in_specs, out_specs=P(ROWS, COLS, None, None), check_vma=False)
```

```python
import functools

import jax
import jax.numpy as jnp
import numpy as np
from jax import lax
from jax.experimental import pallas as pl
from jax.experimental.pallas import tpu as pltpu
from jax.sharding import Mesh
from jax.sharding import PartitionSpec as P

AXES = ("x", "zl", "core", "zh", "y")
ROWS = ("x", "zl", "core")
COLS = ("zh", "y")
CHIPS = ("x", "zl")
VMEM = pltpu.CompilerParams(vmem_limit_bytes=40 * 1024 * 1024)
F32 = jnp.float32
BF16 = jnp.bfloat16
NT = (((1,), (1,)), ((), ()))
TN = (((0,), (0,)), ((), ()))


def _one_hot(source_of):
    source_of = np.asarray(source_of).reshape(-1)
    size = source_of.size
    out = np.zeros((size, size), np.float32)
    out[np.arange(size), source_of] = 1
    return out


def _grid(*sizes):
    return np.meshgrid(*[np.arange(s) for s in sizes], indexing="ij")


def _tables():
    j, h = _grid(32, 2)
    rows = _one_hot(h * 32 + j)
    small = np.stack([rows, rows.T, np.eye(64, dtype=np.float32)])
    row, col, k = _grid(16, 16, 4)
    wide = _one_hot(col * 64 + row * 4 + k).T
    row, col, k = _grid(4, 16, 4)
    rows_b = _one_hot(col * 16 + row * 4 + k)
    h, row, k = _grid(2, 16, 4)
    halves = _one_hot((row * 2 + h) * 4 + k)
    return [np.asarray(t, jnp.bfloat16) for t in (small, wide, rows_b, halves)]


def _chip():
    return lax.axis_index("x") * 2 + lax.axis_index("zl")


def _perm(left, right):
    return jnp.dot(left, right, preferred_element_type=F32).astype(BF16)


def _unpack(part):
    return jnp.concatenate([part[:, :64], part[:, 64:]], axis=0)


def _pack(piece):
    return jnp.concatenate([piece[:32], piece[32:]], axis=1)


def _spread_kernel(fac_ref, out_ref, wide_ref, send_ref, sems):
    wide_ref[:, :4, :] = fac_ref[:, :, :512].astype(F32)
    wide_ref[:, 4:, :] = fac_ref[:, :, 512:].astype(F32)
    send_ref[...] = wide_ref[...].astype(BF16)
    copies = [pltpu.make_async_copy(send_ref, out_ref.at[k * 16 : k * 16 + 16], sems.at[k]) for k in range(4)]
    for copy in copies:
        copy.start()
    for copy in copies:
        copy.wait()


def _mask_kernel(
    amps_ref,
    source_ref,
    screen_ref,
    held_ref,
    mask_ref,
    out0,
    out1,
    out2,
    out3,
    flat_ref,
    flat2_ref,
):
    block = screen_ref[_chip()].astype(F32)
    lane_block = (lax.broadcasted_iota(jnp.int32, (8, 128), 1) % 64) // 8
    spread = (lax.broadcasted_iota(jnp.int32, (8, 128), 0) == lane_block).astype(F32)
    mask = lax.dot_general(block, spread, TN, preferred_element_type=F32)
    mask_ref[...] = mask
    y = lax.axis_index("y")
    for j in range(32):
        tile = slice(j * 128, (j + 1) * 128)
        flat_ref[pl.ds(j, 16, stride=32), :] = amps_ref[:, tile].astype(F32) * mask
        flat2_ref[pl.ds(j, 16, stride=32), :] = source_ref[:, tile].astype(F32)
    for pair in range(16):
        held_ref[pair, :32] = flat_ref[pair * 32 : pair * 32 + 32, :].astype(BF16)
        held_ref[pair, 32:] = flat2_ref[pair * 32 : pair * 32 + 32, :].astype(BF16)
    for k, out in enumerate((out0, out1, out2, out3)):
        to = (y + k) % 4
        for zh in range(4):
            rows = pl.ds(pl.multiple_of(zh * 128 + to * 32, 32), 32)
            turned = pl.ds(pl.multiple_of(to * 128 + zh * 32, 32), 32)
            out[zh, :32, :] = flat_ref[rows, :].astype(BF16)
            out[zh, 32:64, :] = flat_ref[turned, :].astype(BF16)
            out[zh, 64:, :] = flat2_ref[turned, :].astype(BF16)


def _relay_kernel(in0, in1, in2, in3, out0, out1, out2, out3):
    zh, y = lax.axis_index("zh"), lax.axis_index("y")
    for m, out in enumerate((out0, out1, out2, out3)):
        for k, ref in enumerate((in0, in1, in2, in3)):
            out[(y + 4 - k) % 4] = ref[(zh + m) % 4]


def _block_kernel(in0, in1, in2, in3, small_ref, wide_ref, amp_ref, sent_ref, got_ref):
    zh = lax.axis_index("zh")
    for m, ref in enumerate((in0, in1, in2, in3)):
        got_ref[(zh + 4 - m) % 4] = ref[...]

    def block(offset):
        parts = [_unpack(got_ref[c // 4, c % 4, offset : offset + 32, :]) for c in range(16)]
        return _perm(small_ref[0], jnp.concatenate(parts, axis=1))

    whole = jnp.concatenate([block(0), block(32), block(64)], axis=0)
    whole = _perm(whole, wide_ref[...])
    amp_ref[...] = whole[:64]
    for row in range(16):
        cols = slice(row * 64, row * 64 + 64)
        sent_ref[row, :32, :] = _pack(whole[64:128, cols])
        sent_ref[row, 32:, :] = _pack(whole[128:, cols])


def _symmetric_kernel(
    got_ref, amp_ref, small_ref, wide_ref, near_ref, far_ref, last_ref, sent_ref, kept_ref
):
    del near_ref, far_ref, last_ref

    def turned(offset):
        tall = jnp.concatenate([_unpack(got_ref[row, offset : offset + 32, :]) for row in range(16)], axis=0)
        return lax.dot_general(small_ref[2], tall, NT, preferred_element_type=F32)

    block = (amp_ref[...].astype(F32) + turned(0)).astype(BF16)
    for to in range(8):
        sent_ref[to] = block
    source = turned(32).astype(BF16)
    kept_ref[...] = lax.dot_general(source, wide_ref[...], NT, preferred_element_type=F32).astype(BF16)


def _gate_kernel(value_ref, small_ref, out_ref):
    del value_ref, small_ref, out_ref


def _factor_kernel(fac0, fac1, fac2, fac3, halves_ref, rows_ref, right_ref, left_ref):
    y = lax.axis_index("y")
    for k, ref in enumerate((fac0, fac1, fac2, fac3)):
        for zh in range(4):
            part = _perm(halves_ref[...], ref[zh])
            right_ref[zh, (y + 4 - k) % 4] = jnp.concatenate([part[:64], part[64:]], axis=1)
    for x in range(4):
        rows = [right_ref[col // 4, col % 4, x * 16 : x * 16 + 16, :] for col in range(16)]
        part = _perm(rows_ref[...], jnp.concatenate(rows, axis=0))
        for zl in range(2):
            for core in range(2):
                at = zl * 128 + core * 64
                left_ref[x * 2 + zl, core] = part[at : at + 64]


def _second_step(left_ref, core, inner_ref, out_ref):
    for x in range(2):
        rows = jnp.concatenate([left_ref[x * 4 + chip, core] for chip in range(4)], axis=0)
        for j in range(4):
            cols = slice(j * 256, j * 256 + 256)
            part = _perm(rows, inner_ref[:, cols])
            for chip in range(4):
                out_ref[x * 4 + chip, :, cols] = part[chip * 64 : chip * 64 + 64]


def _ladder_kernel(own_ref, other_ref, right_ref, left_ref, inner_ref, give_ref):
    core = lax.axis_index("core")
    first = core == 0
    for i in range(4):
        rows = []
        for chip in (2 * i, 2 * i + 1):
            own, other = own_ref[chip], other_ref[chip]
            rows += [jnp.where(first, own, other), jnp.where(first, other, own)]
        rows = jnp.concatenate(rows, axis=0)
        for j in range(4):
            inner_ref[i * 256 : i * 256 + 256, j * 256 : j * 256 + 256] = lax.dot_general(
                rows, right_ref[j].reshape(256, 1024), NT, preferred_element_type=F32
            ).astype(BF16)
    _second_step(left_ref, 1 - core, inner_ref, give_ref)


def _rest_kernel(left_ref, inner_ref, keep_ref):
    _second_step(left_ref, lax.axis_index("core"), inner_ref, keep_ref)


def _sum_kernel(part_ref, kept_ref, small_ref, sent_ref):
    total = kept_ref[...].astype(F32)
    for chip in range(8):
        total += part_ref[chip].astype(F32)
    total = _perm(small_ref[1], total.astype(BF16))
    for col in range(16):
        sent_ref[col] = _pack(total[:, col * 64 : col * 64 + 64])


def _update_kernel(occ_ref, resid_ref, held_ref, mask_ref, vir_ref, out_ref, flat_ref):
    row = _chip() * 2 + lax.axis_index("core")
    col = lax.axis_index("zh") * 4 + lax.axis_index("y")
    exact = lax.Precision.HIGHEST

    def iota(shape, dim):
        return lax.broadcasted_iota(jnp.int32, shape, dim)

    mine = vir_ref[pl.ds(row // 2, 1), :]
    l_row = iota((32, 128), 1) - (row % 2) * 64
    in_row = (l_row // 2 == iota((32, 128), 0)) & (l_row >= 0)
    picked = jnp.where(in_row, jnp.broadcast_to(mine, (32, 128)), 0.0)
    same_half = (iota((128, 128), 0) % 2 == iota((128, 128), 1) // 64).astype(F32)
    vir_a = jnp.dot(picked, same_half, precision=exact, preferred_element_type=F32)
    lane = iota((128, 128), 1)
    want = ((lane // 4) % 2) * 64 + col * 4 + lane % 4
    choose = (iota((128, 128), 0) == want).astype(F32)
    by_block = jnp.dot(vir_ref[...], choose, precision=exact, preferred_element_type=F32)
    own_block = iota((8, 128), 0) == (iota((8, 128), 1) % 64) // 8
    vir_b = jnp.sum(jnp.where(own_block, by_block, 0.0), axis=0, keepdims=True)
    vir = vir_a + vir_b
    for pair in range(16):
        i, j = pair // 4, pair % 4
        denom = (occ_ref[i] + occ_ref[j]) - vir
        rsym = resid_ref[pair].astype(F32) + held_ref[pair, 32:].astype(F32)
        old = held_ref[pair, :32].astype(F32)
        flat_ref[pair * 32 : pair * 32 + 32, :] = old + mask_ref[pair : pair + 1, :] * (rsym / denom)
    for j in range(32):
        out_ref[:, j * 128 : (j + 1) * 128] = flat_ref[pl.ds(j, 16, stride=32), :].astype(BF16)


def _vmem():
    return pl.BlockSpec(memory_space=pltpu.VMEM)


SMEM = pl.BlockSpec(memory_space=pltpu.SMEM)
HBM = pl.BlockSpec(memory_space=pltpu.HBM)
ANY = pl.BlockSpec(memory_space=pl.ANY)


def _sds(*shape, dtype=BF16):
    return jax.ShapeDtypeStruct(shape, dtype)


def _turn(value, axis, step):
    if step == 0:
        return value
    return lax.ppermute(value, axis, [(i, (i + step) % 4) for i in range(4)])


def _swap_cores(value):
    return lax.ppermute(value, "core", [(0, 1), (1, 0)])


def _after(value, small):
    return pl.pallas_call(
        _gate_kernel,
        out_shape=jax.ShapeDtypeStruct(value.shape, value.dtype),
        in_specs=[_vmem(), ANY],
        out_specs=_vmem(),
        input_output_aliases={0: 0},
        name="gate",
    )(value, small)


def _shards(tables, amps, source, factors, screen, occ_energy, vir_energy):
    small, wide, rows_b, halves = tables
    spread = pl.pallas_call(
        _spread_kernel,
        out_shape=_sds(64, 8, 512),
        in_specs=[_vmem()],
        out_specs=HBM,
        scratch_shapes=[pltpu.VMEM((16, 8, 512), F32), pltpu.VMEM((16, 8, 512), BF16)]
        + [pltpu.SemaphoreType.DMA((4,))],
        name="spread_factors",
    )(factors)
    fac = lax.all_to_all(spread, ("zh",) + ROWS, 0, 0, tiled=True).reshape(4, 128, 512)
    four = _sds(4, 96, 128)
    held, mask, *outs = pl.pallas_call(
        _mask_kernel,
        out_shape=(_sds(16, 64, 128), _sds(16, 128, dtype=F32)) + (four,) * 4,
        in_specs=[_vmem()] * 3,
        out_specs=(_vmem(),) * 6,
        scratch_shapes=[pltpu.VMEM((512, 128), F32)] * 2,
        name="mask_amps",
    )(amps.reshape(16, 4096), source.reshape(16, 4096), screen.transpose(1, 2, 0))
    outs = [_turn(out, "y", k) for k, out in enumerate(outs)]
    outs = pl.pallas_call(
        _relay_kernel,
        out_shape=(four,) * 4,
        in_specs=[_vmem()] * 4,
        out_specs=(_vmem(),) * 4,
        name="relay",
    )(*outs)
    outs = [_turn(out, "zh", k) for k, out in enumerate(outs)]
    near, far = _turn(fac, "y", 1), _turn(fac, "y", 3)
    opposite = _turn(fac, "y", 2)
    block, turn = pl.pallas_call(
        _block_kernel,
        out_shape=(_sds(64, 1024), _sds(16, 64, 128)),
        in_specs=[_vmem()] * 6,
        out_specs=(_vmem(), _vmem()),
        scratch_shapes=[pltpu.VMEM((4, 4, 96, 128), BF16)],
        compiler_params=VMEM,
        name="make_block",
    )(*outs, small, wide)
    turn = lax.all_to_all(turn, ROWS, 0, 0, tiled=True)
    block, kept = pl.pallas_call(
        _symmetric_kernel,
        out_shape=(_sds(8, 64, 1024), _sds(64, 1024)),
        in_specs=[_vmem()] * 4 + [ANY] * 3,
        out_specs=(_vmem(), _vmem()),
        compiler_params=VMEM,
        name="symmetrize",
    )(turn, block, small, wide, near, far, opposite)
    own = lax.all_to_all(block, CHIPS, 0, 0, tiled=True)
    other = _swap_cores(own)
    right, left = pl.pallas_call(
        _factor_kernel,
        out_shape=(_sds(4, 4, 64, 1024), _sds(8, 2, 64, 1024)),
        in_specs=[_vmem()] * 6,
        out_specs=(_vmem(), _vmem()),
        compiler_params=VMEM,
        name="prepare_factors",
    )(fac, near, opposite, far, halves, rows_b)
    inner, give = pl.pallas_call(
        _ladder_kernel,
        out_shape=(_sds(1024, 1024), _sds(8, 64, 1024)),
        in_specs=[_vmem()] * 4,
        out_specs=(_vmem(), _vmem()),
        compiler_params=VMEM,
        name="ladder",
    )(own, other, right, left)
    keep = pl.pallas_call(
        _rest_kernel,
        out_shape=_sds(8, 64, 1024),
        in_specs=[_vmem()] * 2,
        out_specs=_vmem(),
        compiler_params=VMEM,
        name="ladder_rest",
    )(left, inner)
    taken = _swap_cores(give)
    partial = (keep.astype(F32) + taken.astype(F32)).astype(BF16)
    parts = lax.all_to_all(partial, CHIPS, 0, 0, tiled=True)
    last = pl.pallas_call(
        _sum_kernel,
        out_shape=_sds(16, 32, 128),
        in_specs=[_vmem()] * 3,
        out_specs=_vmem(),
        compiler_params=VMEM,
        name="sum_parts",
    )(parts, kept, small)
    back = lax.all_to_all(last, COLS, 0, 0, tiled=True)
    out = pl.pallas_call(
        _update_kernel,
        out_shape=_sds(16, 4096),
        in_specs=[SMEM, _vmem(), _vmem(), _vmem(), _vmem()],
        out_specs=_vmem(),
        scratch_shapes=[pltpu.VMEM((512, 128), F32)],
        name="update",
    )(occ_energy, back, held, mask, vir_energy.reshape(8, 128))
    return out.reshape(1, 1, 16, 4096)


def solution(mesh):
    fine = Mesh(mesh.devices.reshape(4, 2, 2, 4, 4), AXES)
    in_specs = (
        P(ROWS, COLS, None, None),
        P(ROWS, COLS, None, None),
        P(None, ROWS + COLS, None),
        P(),
        P(),
        P(),
    )
    shards = functools.partial(_shards, _tables())
    return jax.shard_map(shards, mesh=fine, in_specs=in_specs, out_specs=P(ROWS, COLS, None, None), check_vma=False)
```

```python
import functools

import jax
import jax.numpy as jnp
import numpy as np
from jax import lax
from jax.experimental import pallas as pl
from jax.experimental.pallas import tpu as pltpu
from jax.sharding import Mesh
from jax.sharding import PartitionSpec as P

AXES = ("x", "zl", "core", "zh", "y")
ROWS = ("x", "zl", "core")
COLS = ("zh", "y")
CHIPS = ("x", "zl")
VMEM = pltpu.CompilerParams(vmem_limit_bytes=40 * 1024 * 1024)
F32 = jnp.float32
BF16 = jnp.bfloat16
NT = (((1,), (1,)), ((), ()))
TN = (((0,), (0,)), ((), ()))


def _one_hot(source_of):
    source_of = np.asarray(source_of).reshape(-1)
    size = source_of.size
    out = np.zeros((size, size), np.float32)
    out[np.arange(size), source_of] = 1
    return out


def _grid(*sizes):
    return np.meshgrid(*[np.arange(s) for s in sizes], indexing="ij")


def _tables():
    j, h = _grid(32, 2)
    rows = _one_hot(h * 32 + j)
    small = np.stack([rows, rows.T, np.eye(64, dtype=np.float32)])
    row, col, k = _grid(16, 16, 4)
    wide = _one_hot(col * 64 + row * 4 + k).T
    row, col, k = _grid(4, 16, 4)
    rows_b = _one_hot(col * 16 + row * 4 + k)
    h, row, k = _grid(2, 16, 4)
    halves = _one_hot((row * 2 + h) * 4 + k)
    return [np.asarray(t, jnp.bfloat16) for t in (small, wide, rows_b, halves)]


def _chip():
    return lax.axis_index("x") * 2 + lax.axis_index("zl")


def _perm(left, right):
    return jnp.dot(left, right, preferred_element_type=F32).astype(BF16)


def _unpack(part):
    return jnp.concatenate([part[:, :64], part[:, 64:]], axis=0)


def _pack(piece):
    return jnp.concatenate([piece[:32], piece[32:]], axis=1)


def _spread_kernel(fac_ref, out_ref, wide_ref, send_ref, sems):
    wide_ref[:, :4, :] = fac_ref[:, :, :512].astype(F32)
    wide_ref[:, 4:, :] = fac_ref[:, :, 512:].astype(F32)
    send_ref[...] = wide_ref[...].astype(BF16)
    copies = [pltpu.make_async_copy(send_ref, out_ref.at[k * 16 : k * 16 + 16], sems.at[k]) for k in range(4)]
    for copy in copies:
        copy.start()
    for copy in copies:
        copy.wait()


def _mask_kernel(
    amps_ref,
    source_ref,
    screen_ref,
    held_ref,
    mask_ref,
    out0,
    out1,
    out2,
    out3,
    flat_ref,
    flat2_ref,
):
    block = screen_ref[_chip()].astype(F32)
    lane_block = (lax.broadcasted_iota(jnp.int32, (8, 128), 1) % 64) // 8
    spread = (lax.broadcasted_iota(jnp.int32, (8, 128), 0) == lane_block).astype(F32)
    mask = lax.dot_general(block, spread, TN, preferred_element_type=F32)
    mask_ref[...] = mask
    y = lax.axis_index("y")
    for j in range(32):
        tile = slice(j * 128, (j + 1) * 128)
        flat_ref[pl.ds(j, 16, stride=32), :] = amps_ref[:, tile].astype(F32) * mask
        flat2_ref[pl.ds(j, 16, stride=32), :] = source_ref[:, tile].astype(F32)
    for pair in range(16):
        held_ref[pair, :32] = flat_ref[pair * 32 : pair * 32 + 32, :].astype(BF16)
        held_ref[pair, 32:] = flat2_ref[pair * 32 : pair * 32 + 32, :].astype(BF16)
    for k, out in enumerate((out0, out1, out2, out3)):
        to = (y + k) % 4
        for zh in range(4):
            rows = pl.ds(pl.multiple_of(zh * 128 + to * 32, 32), 32)
            turned = pl.ds(pl.multiple_of(to * 128 + zh * 32, 32), 32)
            out[zh, :32, :] = flat_ref[rows, :].astype(BF16)
            out[zh, 32:64, :] = flat_ref[turned, :].astype(BF16)
            out[zh, 64:, :] = flat2_ref[turned, :].astype(BF16)


def _relay_kernel(in0, in1, in2, in3, out0, out1, out2, out3):
    zh, y = lax.axis_index("zh"), lax.axis_index("y")
    for m, out in enumerate((out0, out1, out2, out3)):
        for k, ref in enumerate((in0, in1, in2, in3)):
            out[(y + 4 - k) % 4] = ref[(zh + m) % 4]


def _block_kernel(in0, in1, in2, in3, small_ref, wide_ref, amp_ref, sent_ref, got_ref):
    zh = lax.axis_index("zh")
    for m, ref in enumerate((in0, in1, in2, in3)):
        got_ref[(zh + 4 - m) % 4] = ref[...]

    def block(offset):
        parts = [_unpack(got_ref[c // 4, c % 4, offset : offset + 32, :]) for c in range(16)]
        return _perm(small_ref[0], jnp.concatenate(parts, axis=1))

    whole = jnp.concatenate([block(0), block(32), block(64)], axis=0)
    whole = _perm(whole, wide_ref[...])
    amp_ref[...] = whole[:64]
    for row in range(16):
        cols = slice(row * 64, row * 64 + 64)
        sent_ref[row, :32, :] = _pack(whole[64:128, cols])
        sent_ref[row, 32:, :] = _pack(whole[128:, cols])


def _symmetric_kernel(
    got_ref, amp_ref, small_ref, wide_ref, near_ref, far_ref, last_ref, sent_ref, kept_ref
):
    del near_ref, far_ref, last_ref

    def turned(offset):
        tall = jnp.concatenate([_unpack(got_ref[row, offset : offset + 32, :]) for row in range(16)], axis=0)
        return lax.dot_general(small_ref[2], tall, NT, preferred_element_type=F32)

    block = (amp_ref[...].astype(F32) + turned(0)).astype(BF16)
    for to in range(8):
        sent_ref[to] = block
    source = turned(32).astype(BF16)
    kept_ref[...] = lax.dot_general(source, wide_ref[...], NT, preferred_element_type=F32).astype(BF16)


def _gate_kernel(value_ref, small_ref, out_ref):
    del value_ref, small_ref, out_ref


def _factor_kernel(fac0, fac1, fac2, fac3, halves_ref, rows_ref, right_ref, left_ref):
    y = lax.axis_index("y")
    for k, ref in enumerate((fac0, fac1, fac2, fac3)):
        for zh in range(4):
            part = _perm(halves_ref[...], ref[zh])
            right_ref[zh, (y + 4 - k) % 4] = jnp.concatenate([part[:64], part[64:]], axis=1)
    for x in range(4):
        rows = [right_ref[col // 4, col % 4, x * 16 : x * 16 + 16, :] for col in range(16)]
        part = _perm(rows_ref[...], jnp.concatenate(rows, axis=0))
        for zl in range(2):
            for core in range(2):
                at = zl * 128 + core * 64
                left_ref[x * 2 + zl, core] = part[at : at + 64]


def _second_step(left_ref, core, inner_ref, out_ref):
    for x in range(2):
        rows = jnp.concatenate([left_ref[x * 4 + chip, core] for chip in range(4)], axis=0)
        for j in range(4):
            cols = slice(j * 256, j * 256 + 256)
            part = _perm(rows, inner_ref[:, cols])
            for chip in range(4):
                out_ref[x * 4 + chip, :, cols] = part[chip * 64 : chip * 64 + 64]


def _first_step(amp_ref, right_ref, put):
    for i in range(2):
        rows = amp_ref[i * 4 : i * 4 + 4].reshape(256, 1024)
        for j in range(4):
            part = lax.dot_general(rows, right_ref[j].reshape(256, 1024), NT, preferred_element_type=F32)
            put(i, slice(j * 256, j * 256 + 256), part.astype(BF16))


def _own_kernel(own_ref, right_ref, part_ref):
    def put(i, cols, part):
        part_ref[i * 4 : i * 4 + 4, :, cols] = part.reshape(4, 64, 256)

    _first_step(own_ref, right_ref, put)


def _ladder_kernel(other_ref, right_ref, left_ref, part_ref, inner_ref, give_ref):
    core = lax.axis_index("core")
    first = core == 0

    def put(i, cols, part):
        for chip in range(4):
            own, other = part_ref[i * 4 + chip, :, cols], part[chip * 64 : chip * 64 + 64]
            at = (i * 4 + chip) * 128
            inner_ref[at : at + 64, cols] = jnp.where(first, own, other)
            inner_ref[at + 64 : at + 128, cols] = jnp.where(first, other, own)

    _first_step(other_ref, right_ref, put)
    _second_step(left_ref, 1 - core, inner_ref, give_ref)


def _rest_kernel(left_ref, inner_ref, keep_ref):
    _second_step(left_ref, lax.axis_index("core"), inner_ref, keep_ref)


def _sum_kernel(part_ref, kept_ref, small_ref, sent_ref):
    total = kept_ref[...].astype(F32)
    for chip in range(8):
        total += part_ref[chip].astype(F32)
    total = _perm(small_ref[1], total.astype(BF16))
    for col in range(16):
        sent_ref[col] = _pack(total[:, col * 64 : col * 64 + 64])


def _update_kernel(occ_ref, resid_ref, held_ref, mask_ref, vir_ref, out_ref, flat_ref):
    row = _chip() * 2 + lax.axis_index("core")
    col = lax.axis_index("zh") * 4 + lax.axis_index("y")
    exact = lax.Precision.HIGHEST

    def iota(shape, dim):
        return lax.broadcasted_iota(jnp.int32, shape, dim)

    mine = vir_ref[pl.ds(row // 2, 1), :]
    l_row = iota((32, 128), 1) - (row % 2) * 64
    in_row = (l_row // 2 == iota((32, 128), 0)) & (l_row >= 0)
    picked = jnp.where(in_row, jnp.broadcast_to(mine, (32, 128)), 0.0)
    same_half = (iota((128, 128), 0) % 2 == iota((128, 128), 1) // 64).astype(F32)
    vir_a = jnp.dot(picked, same_half, precision=exact, preferred_element_type=F32)
    lane = iota((128, 128), 1)
    want = ((lane // 4) % 2) * 64 + col * 4 + lane % 4
    choose = (iota((128, 128), 0) == want).astype(F32)
    by_block = jnp.dot(vir_ref[...], choose, precision=exact, preferred_element_type=F32)
    own_block = iota((8, 128), 0) == (iota((8, 128), 1) % 64) // 8
    vir_b = jnp.sum(jnp.where(own_block, by_block, 0.0), axis=0, keepdims=True)
    vir = vir_a + vir_b
    for pair in range(16):
        i, j = pair // 4, pair % 4
        denom = (occ_ref[i] + occ_ref[j]) - vir
        rsym = resid_ref[pair].astype(F32) + held_ref[pair, 32:].astype(F32)
        old = held_ref[pair, :32].astype(F32)
        flat_ref[pair * 32 : pair * 32 + 32, :] = old + mask_ref[pair : pair + 1, :] * (rsym / denom)
    for j in range(32):
        out_ref[:, j * 128 : (j + 1) * 128] = flat_ref[pl.ds(j, 16, stride=32), :].astype(BF16)


def _vmem():
    return pl.BlockSpec(memory_space=pltpu.VMEM)


SMEM = pl.BlockSpec(memory_space=pltpu.SMEM)
HBM = pl.BlockSpec(memory_space=pltpu.HBM)
ANY = pl.BlockSpec(memory_space=pl.ANY)


def _sds(*shape, dtype=BF16):
    return jax.ShapeDtypeStruct(shape, dtype)


def _turn(value, axis, step):
    if step == 0:
        return value
    return lax.ppermute(value, axis, [(i, (i + step) % 4) for i in range(4)])


def _swap_cores(value):
    return lax.ppermute(value, "core", [(0, 1), (1, 0)])


def _after(value, small):
    return pl.pallas_call(
        _gate_kernel,
        out_shape=jax.ShapeDtypeStruct(value.shape, value.dtype),
        in_specs=[_vmem(), ANY],
        out_specs=_vmem(),
        input_output_aliases={0: 0},
        name="gate",
    )(value, small)


def _shards(tables, amps, source, factors, screen, occ_energy, vir_energy):
    small, wide, rows_b, halves = tables
    spread = pl.pallas_call(
        _spread_kernel,
        out_shape=_sds(64, 8, 512),
        in_specs=[_vmem()],
        out_specs=HBM,
        scratch_shapes=[pltpu.VMEM((16, 8, 512), F32), pltpu.VMEM((16, 8, 512), BF16)]
        + [pltpu.SemaphoreType.DMA((4,))],
        name="spread_factors",
    )(factors)
    fac = lax.all_to_all(spread, ("zh",) + ROWS, 0, 0, tiled=True).reshape(4, 128, 512)
    four = _sds(4, 96, 128)
    held, mask, *outs = pl.pallas_call(
        _mask_kernel,
        out_shape=(_sds(16, 64, 128), _sds(16, 128, dtype=F32)) + (four,) * 4,
        in_specs=[_vmem()] * 3,
        out_specs=(_vmem(),) * 6,
        scratch_shapes=[pltpu.VMEM((512, 128), F32)] * 2,
        name="mask_amps",
    )(amps.reshape(16, 4096), source.reshape(16, 4096), screen.transpose(1, 2, 0))
    outs = [_turn(out, "y", k) for k, out in enumerate(outs)]
    outs = pl.pallas_call(
        _relay_kernel,
        out_shape=(four,) * 4,
        in_specs=[_vmem()] * 4,
        out_specs=(_vmem(),) * 4,
        name="relay",
    )(*outs)
    outs = [_turn(out, "zh", k) for k, out in enumerate(outs)]
    near, far = _turn(fac, "y", 1), _turn(fac, "y", 3)
    opposite = _turn(fac, "y", 2)
    block, turn = pl.pallas_call(
        _block_kernel,
        out_shape=(_sds(64, 1024), _sds(16, 64, 128)),
        in_specs=[_vmem()] * 6,
        out_specs=(_vmem(), _vmem()),
        scratch_shapes=[pltpu.VMEM((4, 4, 96, 128), BF16)],
        compiler_params=VMEM,
        name="make_block",
    )(*outs, small, wide)
    turn = lax.all_to_all(turn, ROWS, 0, 0, tiled=True)
    block, kept = pl.pallas_call(
        _symmetric_kernel,
        out_shape=(_sds(8, 64, 1024), _sds(64, 1024)),
        in_specs=[_vmem()] * 4 + [ANY] * 3,
        out_specs=(_vmem(), _vmem()),
        compiler_params=VMEM,
        name="symmetrize",
    )(turn, block, small, wide, near, far, opposite)
    own = lax.all_to_all(block, CHIPS, 0, 0, tiled=True)
    other = _swap_cores(own)
    right, left = pl.pallas_call(
        _factor_kernel,
        out_shape=(_sds(4, 4, 64, 1024), _sds(8, 2, 64, 1024)),
        in_specs=[_vmem()] * 6,
        out_specs=(_vmem(), _vmem()),
        compiler_params=VMEM,
        name="prepare_factors",
    )(fac, near, opposite, far, halves, rows_b)
    part = pl.pallas_call(
        _own_kernel,
        out_shape=_sds(8, 64, 1024),
        in_specs=[_vmem()] * 2,
        out_specs=_vmem(),
        compiler_params=VMEM,
        name="ladder_own",
    )(own, right)
    inner, give = pl.pallas_call(
        _ladder_kernel,
        out_shape=(_sds(1024, 1024), _sds(8, 64, 1024)),
        in_specs=[_vmem()] * 4,
        out_specs=(_vmem(), _vmem()),
        compiler_params=VMEM,
        name="ladder",
    )(other, right, left, part)
    keep = pl.pallas_call(
        _rest_kernel,
        out_shape=_sds(8, 64, 1024),
        in_specs=[_vmem()] * 2,
        out_specs=_vmem(),
        compiler_params=VMEM,
        name="ladder_rest",
    )(left, inner)
    taken = _swap_cores(give)
    partial = (keep.astype(F32) + taken.astype(F32)).astype(BF16)
    parts = lax.all_to_all(partial, CHIPS, 0, 0, tiled=True)
    last = pl.pallas_call(
        _sum_kernel,
        out_shape=_sds(16, 32, 128),
        in_specs=[_vmem()] * 3,
        out_specs=_vmem(),
        compiler_params=VMEM,
        name="sum_parts",
    )(parts, kept, small)
    back = lax.all_to_all(last, COLS, 0, 0, tiled=True)
    out = pl.pallas_call(
        _update_kernel,
        out_shape=_sds(16, 4096),
        in_specs=[SMEM, _vmem(), _vmem(), _vmem(), _vmem()],
        out_specs=_vmem(),
        scratch_shapes=[pltpu.VMEM((512, 128), F32)],
        name="update",
    )(occ_energy, back, held, mask, vir_energy.reshape(8, 128))
    return out.reshape(1, 1, 16, 4096)


def solution(mesh):
    fine = Mesh(mesh.devices.reshape(4, 2, 2, 4, 4), AXES)
    in_specs = (
        P(ROWS, COLS, None, None),
        P(ROWS, COLS, None, None),
        P(None, ROWS + COLS, None),
        P(),
        P(),
        P(),
    )
    shards = functools.partial(_shards, _tables())
    return jax.shard_map(shards, mesh=fine, in_specs=in_specs, out_specs=P(ROWS, COLS, None, None), check_vma=False)
```

```python
import functools

import jax
import jax.numpy as jnp
import numpy as np
from jax import lax
from jax.experimental import pallas as pl
from jax.experimental.pallas import tpu as pltpu
from jax.sharding import Mesh
from jax.sharding import PartitionSpec as P

AXES = ("x", "zl", "core", "zh", "y")
ROWS = ("x", "zl", "core")
COLS = ("zh", "y")
CHIPS = ("x", "zl")
VMEM = pltpu.CompilerParams(vmem_limit_bytes=40 * 1024 * 1024)
F32 = jnp.float32
BF16 = jnp.bfloat16
NT = (((1,), (1,)), ((), ()))
TN = (((0,), (0,)), ((), ()))


def _one_hot(source_of):
    source_of = np.asarray(source_of).reshape(-1)
    size = source_of.size
    out = np.zeros((size, size), np.float32)
    out[np.arange(size), source_of] = 1
    return out


def _grid(*sizes):
    return np.meshgrid(*[np.arange(s) for s in sizes], indexing="ij")


def _tables():
    j, h = _grid(32, 2)
    rows = _one_hot(h * 32 + j)
    small = np.stack([rows, rows.T, np.eye(64, dtype=np.float32)])
    row, col, k = _grid(16, 16, 4)
    wide = _one_hot(col * 64 + row * 4 + k).T
    row, col, k = _grid(4, 16, 4)
    rows_b = _one_hot(col * 16 + row * 4 + k)
    h, row, k = _grid(2, 16, 4)
    halves = _one_hot((row * 2 + h) * 4 + k)
    return [np.asarray(t, jnp.bfloat16) for t in (small, wide, rows_b, halves)]


def _chip():
    return lax.axis_index("x") * 2 + lax.axis_index("zl")


def _perm(left, right):
    return jnp.dot(left, right, preferred_element_type=F32).astype(BF16)


def _unpack(part):
    return jnp.concatenate([part[:, :64], part[:, 64:]], axis=0)


def _pack(piece):
    return jnp.concatenate([piece[:32], piece[32:]], axis=1)


def _spread_kernel(fac_ref, out_ref, wide_ref, send_ref, sems):
    wide_ref[:, :4, :] = fac_ref[:, :, :512].astype(F32)
    wide_ref[:, 4:, :] = fac_ref[:, :, 512:].astype(F32)
    send_ref[...] = wide_ref[...].astype(BF16)
    copies = [pltpu.make_async_copy(send_ref, out_ref.at[k * 16 : k * 16 + 16], sems.at[k]) for k in range(4)]
    for copy in copies:
        copy.start()
    for copy in copies:
        copy.wait()


def _mask_kernel(
    amps_ref,
    source_ref,
    screen_ref,
    held_ref,
    mask_ref,
    out0,
    out1,
    out2,
    out3,
    flat_ref,
    flat2_ref,
):
    block = screen_ref[_chip()].astype(F32)
    lane_block = (lax.broadcasted_iota(jnp.int32, (8, 128), 1) % 64) // 8
    spread = (lax.broadcasted_iota(jnp.int32, (8, 128), 0) == lane_block).astype(F32)
    mask = lax.dot_general(block, spread, TN, preferred_element_type=F32)
    mask_ref[...] = mask
    y = lax.axis_index("y")
    for j in range(32):
        tile = slice(j * 128, (j + 1) * 128)
        flat_ref[pl.ds(j, 16, stride=32), :] = amps_ref[:, tile].astype(F32) * mask
        flat2_ref[pl.ds(j, 16, stride=32), :] = source_ref[:, tile].astype(F32)
    for pair in range(16):
        held_ref[pair, :32] = flat_ref[pair * 32 : pair * 32 + 32, :].astype(BF16)
        held_ref[pair, 32:] = flat2_ref[pair * 32 : pair * 32 + 32, :].astype(BF16)
    for k, out in enumerate((out0, out1, out2, out3)):
        to = (y + k) % 4
        for zh in range(4):
            rows = pl.ds(pl.multiple_of(zh * 128 + to * 32, 32), 32)
            turned = pl.ds(pl.multiple_of(to * 128 + zh * 32, 32), 32)
            out[zh, :32, :] = flat_ref[rows, :].astype(BF16)
            out[zh, 32:64, :] = flat_ref[turned, :].astype(BF16)
            out[zh, 64:, :] = flat2_ref[turned, :].astype(BF16)


def _relay_kernel(in0, in1, in2, in3, out0, out1, out2, out3):
    zh, y = lax.axis_index("zh"), lax.axis_index("y")
    for m, out in enumerate((out0, out1, out2, out3)):
        for k, ref in enumerate((in0, in1, in2, in3)):
            out[(y + 4 - k) % 4] = ref[(zh + m) % 4]


def _block_kernel(in0, in1, in2, in3, small_ref, wide_ref, amp_ref, sent_ref, got_ref):
    zh = lax.axis_index("zh")
    for m, ref in enumerate((in0, in1, in2, in3)):
        got_ref[(zh + 4 - m) % 4] = ref[...]

    def block(offset):
        parts = [_unpack(got_ref[c // 4, c % 4, offset : offset + 32, :]) for c in range(16)]
        return _perm(small_ref[0], jnp.concatenate(parts, axis=1))

    whole = jnp.concatenate([block(0), block(32), block(64)], axis=0)
    whole = _perm(whole, wide_ref[...])
    amp_ref[...] = whole[:64]
    for row in range(16):
        cols = slice(row * 64, row * 64 + 64)
        sent_ref[row, :32, :] = _pack(whole[64:128, cols])
        sent_ref[row, 32:, :] = _pack(whole[128:, cols])


def _symmetric_kernel(
    got_ref, amp_ref, small_ref, wide_ref, near_ref, far_ref, last_ref, sent_ref, kept_ref
):
    del near_ref, far_ref, last_ref

    def turned(offset):
        tall = jnp.concatenate([_unpack(got_ref[row, offset : offset + 32, :]) for row in range(16)], axis=0)
        return lax.dot_general(small_ref[2], tall, NT, preferred_element_type=F32)

    block = (amp_ref[...].astype(F32) + turned(0)).astype(BF16)
    for to in range(8):
        sent_ref[to] = block
    source = turned(32).astype(BF16)
    kept_ref[...] = lax.dot_general(source, wide_ref[...], NT, preferred_element_type=F32).astype(BF16)


def _factor_kernel(fac0, fac1, fac2, fac3, halves_ref, rows_ref, right_ref, left_ref):
    y = lax.axis_index("y")
    for k, ref in enumerate((fac0, fac1, fac2, fac3)):
        for zh in range(4):
            part = _perm(halves_ref[...], ref[zh])
            right_ref[zh, (y + 4 - k) % 4] = jnp.concatenate([part[:64], part[64:]], axis=1)
    for x in range(4):
        rows = [right_ref[col // 4, col % 4, x * 16 : x * 16 + 16, :] for col in range(16)]
        part = _perm(rows_ref[...], jnp.concatenate(rows, axis=0))
        for zl in range(2):
            for core in range(2):
                at = zl * 128 + core * 64
                left_ref[x * 2 + zl, core] = part[at : at + 64]


def _second_step(left_ref, core, inner_ref, out_ref):
    for x in range(2):
        rows = jnp.concatenate([left_ref[x * 4 + chip, core] for chip in range(4)], axis=0)
        for j in range(4):
            cols = slice(j * 256, j * 256 + 256)
            part = _perm(rows, inner_ref[:, cols])
            for chip in range(4):
                out_ref[x * 4 + chip, :, cols] = part[chip * 64 : chip * 64 + 64]


def _first_step(amp_ref, right_ref, put):
    for i in range(2):
        rows = amp_ref[i * 4 : i * 4 + 4].reshape(256, 1024)
        for j in range(4):
            part = lax.dot_general(rows, right_ref[j].reshape(256, 1024), NT, preferred_element_type=F32)
            put(i, slice(j * 256, j * 256 + 256), part.astype(BF16))


def _own_kernel(own_ref, right_ref, part_ref):
    def put(i, cols, part):
        part_ref[i * 4 : i * 4 + 4, :, cols] = part.reshape(4, 64, 256)

    _first_step(own_ref, right_ref, put)


def _ladder_kernel(other_ref, right_ref, left_ref, part_ref, inner_ref, give_ref):
    core = lax.axis_index("core")
    first = core == 0

    def put(i, cols, part):
        for chip in range(4):
            own, other = part_ref[i * 4 + chip, :, cols], part[chip * 64 : chip * 64 + 64]
            at = (i * 4 + chip) * 128
            inner_ref[at : at + 64, cols] = jnp.where(first, own, other)
            inner_ref[at + 64 : at + 128, cols] = jnp.where(first, other, own)

    _first_step(other_ref, right_ref, put)
    _second_step(left_ref, 1 - core, inner_ref, give_ref)


def _rest_kernel(left_ref, inner_ref, keep_ref):
    _second_step(left_ref, lax.axis_index("core"), inner_ref, keep_ref)


def _sum_kernel(part_ref, kept_ref, small_ref, sent_ref):
    total = kept_ref[...].astype(F32)
    for chip in range(8):
        total += part_ref[chip].astype(F32)
    total = _perm(small_ref[1], total.astype(BF16))
    for col in range(16):
        sent_ref[col] = _pack(total[:, col * 64 : col * 64 + 64])


def _update_kernel(occ_ref, resid_ref, held_ref, mask_ref, vir_ref, out_ref, flat_ref):
    row = _chip() * 2 + lax.axis_index("core")
    col = lax.axis_index("zh") * 4 + lax.axis_index("y")
    exact = lax.Precision.HIGHEST

    def iota(shape, dim):
        return lax.broadcasted_iota(jnp.int32, shape, dim)

    mine = vir_ref[pl.ds(row // 2, 1), :]
    l_row = iota((32, 128), 1) - (row % 2) * 64
    in_row = (l_row // 2 == iota((32, 128), 0)) & (l_row >= 0)
    picked = jnp.where(in_row, jnp.broadcast_to(mine, (32, 128)), 0.0)
    same_half = (iota((128, 128), 0) % 2 == iota((128, 128), 1) // 64).astype(F32)
    vir_a = jnp.dot(picked, same_half, precision=exact, preferred_element_type=F32)
    lane = iota((128, 128), 1)
    want = ((lane // 4) % 2) * 64 + col * 4 + lane % 4
    choose = (iota((128, 128), 0) == want).astype(F32)
    by_block = jnp.dot(vir_ref[...], choose, precision=exact, preferred_element_type=F32)
    own_block = iota((8, 128), 0) == (iota((8, 128), 1) % 64) // 8
    vir_b = jnp.sum(jnp.where(own_block, by_block, 0.0), axis=0, keepdims=True)
    vir = vir_a + vir_b
    for pair in range(16):
        i, j = pair // 4, pair % 4
        denom = (occ_ref[i] + occ_ref[j]) - vir
        rsym = resid_ref[pair].astype(F32) + held_ref[pair, 32:].astype(F32)
        old = held_ref[pair, :32].astype(F32)
        flat_ref[pair * 32 : pair * 32 + 32, :] = old + mask_ref[pair : pair + 1, :] * (rsym / denom)
    for j in range(32):
        out_ref[:, j * 128 : (j + 1) * 128] = flat_ref[pl.ds(j, 16, stride=32), :].astype(BF16)


def _vmem():
    return pl.BlockSpec(memory_space=pltpu.VMEM)


SMEM = pl.BlockSpec(memory_space=pltpu.SMEM)
HBM = pl.BlockSpec(memory_space=pltpu.HBM)
ANY = pl.BlockSpec(memory_space=pl.ANY)


def _sds(*shape, dtype=BF16):
    return jax.ShapeDtypeStruct(shape, dtype)


def _turn(value, axis, step):
    if step == 0:
        return value
    return lax.ppermute(value, axis, [(i, (i + step) % 4) for i in range(4)])


def _swap_cores(value):
    return lax.ppermute(value, "core", [(0, 1), (1, 0)])


def _shards(tables, amps, source, factors, screen, occ_energy, vir_energy):
    small, wide, rows_b, halves = tables
    spread = pl.pallas_call(
        _spread_kernel,
        out_shape=_sds(64, 8, 512),
        in_specs=[_vmem()],
        out_specs=HBM,
        scratch_shapes=[pltpu.VMEM((16, 8, 512), F32), pltpu.VMEM((16, 8, 512), BF16)]
        + [pltpu.SemaphoreType.DMA((4,))],
        name="spread_factors",
    )(factors)
    fac = lax.all_to_all(spread, ("zh",) + ROWS, 0, 0, tiled=True).reshape(4, 128, 512)
    four = _sds(4, 96, 128)
    held, mask, *outs = pl.pallas_call(
        _mask_kernel,
        out_shape=(_sds(16, 64, 128), _sds(16, 128, dtype=F32)) + (four,) * 4,
        in_specs=[_vmem()] * 3,
        out_specs=(_vmem(),) * 6,
        scratch_shapes=[pltpu.VMEM((544, 128), F32)] * 2,
        name="mask_amps",
    )(amps.reshape(16, 4096), source.reshape(16, 4096), screen.transpose(1, 2, 0))
    outs = [_turn(out, "y", k) for k, out in enumerate(outs)]
    outs = pl.pallas_call(
        _relay_kernel,
        out_shape=(four,) * 4,
        in_specs=[_vmem()] * 4,
        out_specs=(_vmem(),) * 4,
        name="relay",
    )(*outs)
    outs = [_turn(out, "zh", k) for k, out in enumerate(outs)]
    near, far = _turn(fac, "y", 1), _turn(fac, "y", 3)
    opposite = _turn(fac, "y", 2)
    block, turn = pl.pallas_call(
        _block_kernel,
        out_shape=(_sds(64, 1024), _sds(16, 64, 128)),
        in_specs=[_vmem()] * 6,
        out_specs=(_vmem(), _vmem()),
        scratch_shapes=[pltpu.VMEM((4, 4, 96, 128), BF16)],
        compiler_params=VMEM,
        name="make_block",
    )(*outs, small, wide)
    turn = lax.all_to_all(turn, ROWS, 0, 0, tiled=True)
    block, kept = pl.pallas_call(
        _symmetric_kernel,
        out_shape=(_sds(8, 64, 1024), _sds(64, 1024)),
        in_specs=[_vmem()] * 4 + [ANY] * 3,
        out_specs=(_vmem(), _vmem()),
        compiler_params=VMEM,
        name="symmetrize",
    )(turn, block, small, wide, near, far, opposite)
    own = lax.all_to_all(block, CHIPS, 0, 0, tiled=True)
    other = _swap_cores(own)
    right, left = pl.pallas_call(
        _factor_kernel,
        out_shape=(_sds(4, 4, 64, 1024), _sds(8, 2, 64, 1024)),
        in_specs=[_vmem()] * 6,
        out_specs=(_vmem(), _vmem()),
        compiler_params=VMEM,
        name="prepare_factors",
    )(fac, near, opposite, far, halves, rows_b)
    part = pl.pallas_call(
        _own_kernel,
        out_shape=_sds(8, 64, 1024),
        in_specs=[_vmem()] * 2,
        out_specs=_vmem(),
        compiler_params=VMEM,
        name="ladder_own",
    )(own, right)
    inner, give = pl.pallas_call(
        _ladder_kernel,
        out_shape=(_sds(1024, 1024), _sds(8, 64, 1024)),
        in_specs=[_vmem()] * 4,
        out_specs=(_vmem(), _vmem()),
        compiler_params=VMEM,
        name="ladder",
    )(other, right, left, part)
    keep = pl.pallas_call(
        _rest_kernel,
        out_shape=_sds(8, 64, 1024),
        in_specs=[_vmem()] * 2,
        out_specs=_vmem(),
        compiler_params=VMEM,
        name="ladder_rest",
    )(left, inner)
    taken = _swap_cores(give)
    partial = (keep.astype(F32) + taken.astype(F32)).astype(BF16)
    parts = lax.all_to_all(partial, CHIPS, 0, 0, tiled=True)
    last = pl.pallas_call(
        _sum_kernel,
        out_shape=_sds(16, 32, 128),
        in_specs=[_vmem()] * 3,
        out_specs=_vmem(),
        compiler_params=VMEM,
        name="sum_parts",
    )(parts, kept, small)
    back = lax.all_to_all(last, COLS, 0, 0, tiled=True)
    out = pl.pallas_call(
        _update_kernel,
        out_shape=_sds(16, 4096),
        in_specs=[SMEM, _vmem(), _vmem(), _vmem(), _vmem()],
        out_specs=_vmem(),
        scratch_shapes=[pltpu.VMEM((544, 128), F32)],
        name="update",
    )(occ_energy, back, held, mask, vir_energy.reshape(8, 128))
    return out.reshape(1, 1, 16, 4096)


def solution(mesh):
    fine = Mesh(mesh.devices.reshape(4, 2, 2, 4, 4), AXES)
    in_specs = (
        P(ROWS, COLS, None, None),
        P(ROWS, COLS, None, None),
        P(None, ROWS + COLS, None),
        P(),
        P(),
        P(),
    )
    shards = functools.partial(_shards, _tables())
    return jax.shard_map(shards, mesh=fine, in_specs=in_specs, out_specs=P(ROWS, COLS, None, None), check_vma=False)
```

```python
import functools

import jax
import jax.numpy as jnp
import numpy as np
from jax import lax
from jax.experimental import pallas as pl
from jax.experimental.pallas import tpu as pltpu
from jax.sharding import Mesh
from jax.sharding import PartitionSpec as P

AXES = ("x", "zl", "core", "zh", "y")
ROWS = ("x", "zl", "core")
COLS = ("zh", "y")
CHIPS = ("x", "zl")
VMEM = pltpu.CompilerParams(vmem_limit_bytes=40 * 1024 * 1024)
F32 = jnp.float32
BF16 = jnp.bfloat16
NT = (((1,), (1,)), ((), ()))
TN = (((0,), (0,)), ((), ()))


def _one_hot(source_of):
    source_of = np.asarray(source_of).reshape(-1)
    size = source_of.size
    out = np.zeros((size, size), np.float32)
    out[np.arange(size), source_of] = 1
    return out


def _grid(*sizes):
    return np.meshgrid(*[np.arange(s) for s in sizes], indexing="ij")


def _tables():
    j, h = _grid(32, 2)
    rows = _one_hot(h * 32 + j)
    small = np.stack([rows, rows.T, np.eye(64, dtype=np.float32)])
    row, col, k = _grid(16, 16, 4)
    wide = _one_hot(col * 64 + row * 4 + k).T
    row, col, k = _grid(4, 16, 4)
    rows_b = _one_hot(col * 16 + row * 4 + k)
    h, row, k = _grid(2, 16, 4)
    halves = _one_hot((row * 2 + h) * 4 + k)
    return [np.asarray(t, jnp.bfloat16) for t in (small, wide, rows_b, halves)]


def _chip():
    return lax.axis_index("x") * 2 + lax.axis_index("zl")


def _perm(left, right):
    return jnp.dot(left, right, preferred_element_type=F32).astype(BF16)


def _unpack(part):
    return jnp.concatenate([part[:, :64], part[:, 64:]], axis=0)


def _pack(piece):
    return jnp.concatenate([piece[:32], piece[32:]], axis=1)


def _spread_kernel(fac_ref, out_ref, wide_ref, send_ref, sems):
    wide_ref[:, :4, :] = fac_ref[:, :, :512].astype(F32)
    wide_ref[:, 4:, :] = fac_ref[:, :, 512:].astype(F32)
    send_ref[...] = wide_ref[...].astype(BF16)
    copies = [pltpu.make_async_copy(send_ref, out_ref.at[k * 16 : k * 16 + 16], sems.at[k]) for k in range(4)]
    for copy in copies:
        copy.start()
    for copy in copies:
        copy.wait()


def _mask_kernel(
    amps_ref,
    source_ref,
    screen_ref,
    held_ref,
    mask_ref,
    out0,
    out1,
    out2,
    out3,
    flat_ref,
    flat2_ref,
):
    block = screen_ref[_chip()].astype(F32)
    lane_block = (lax.broadcasted_iota(jnp.int32, (8, 128), 1) % 64) // 8
    spread = (lax.broadcasted_iota(jnp.int32, (8, 128), 0) == lane_block).astype(F32)
    mask = lax.dot_general(block, spread, TN, preferred_element_type=F32)
    mask_ref[...] = mask
    y = lax.axis_index("y")
    for j in range(32):
        tile = slice(j * 128, (j + 1) * 128)
        flat_ref[pl.ds(j, 16, stride=32), :] = amps_ref[:, tile].astype(F32) * mask
        flat2_ref[pl.ds(j, 16, stride=32), :] = source_ref[:, tile].astype(F32)
    for pair in range(16):
        held_ref[pair, :32] = flat_ref[pair * 32 : pair * 32 + 32, :].astype(BF16)
        held_ref[pair, 32:] = flat2_ref[pair * 32 : pair * 32 + 32, :].astype(BF16)
    for k, out in enumerate((out0, out1, out2, out3)):
        to = (y + k) % 4
        for zh in range(4):
            rows = pl.ds(pl.multiple_of(zh * 128 + to * 32, 32), 32)
            turned = pl.ds(pl.multiple_of(to * 128 + zh * 32, 32), 32)
            out[zh, :32, :] = flat_ref[rows, :].astype(BF16)
            out[zh, 32:64, :] = flat_ref[turned, :].astype(BF16)
            out[zh, 64:, :] = flat2_ref[turned, :].astype(BF16)


def _relay_kernel(in0, in1, in2, in3, out0, out1, out2, out3):
    zh, y = lax.axis_index("zh"), lax.axis_index("y")
    for m, out in enumerate((out0, out1, out2, out3)):
        for k, ref in enumerate((in0, in1, in2, in3)):
            out[(y + 4 - k) % 4] = ref[(zh + m) % 4]


def _block_kernel(in0, in1, in2, in3, small_ref, wide_ref, amp_ref, sent_ref, got_ref):
    zh = lax.axis_index("zh")
    for m, ref in enumerate((in0, in1, in2, in3)):
        got_ref[(zh + 4 - m) % 4] = ref[...]

    def block(offset):
        parts = [_unpack(got_ref[c // 4, c % 4, offset : offset + 32, :]) for c in range(16)]
        return _perm(small_ref[0], jnp.concatenate(parts, axis=1))

    whole = jnp.concatenate([block(0), block(32), block(64)], axis=0)
    whole = _perm(whole, wide_ref[...])
    amp_ref[...] = whole[:64]
    for row in range(16):
        cols = slice(row * 64, row * 64 + 64)
        sent_ref[row, :32, :] = _pack(whole[64:128, cols])
        sent_ref[row, 32:, :] = _pack(whole[128:, cols])


def _symmetric_kernel(got_ref, amp_ref, small_ref, wide_ref, sent_ref, kept_ref):

    def turned(offset):
        tall = jnp.concatenate([_unpack(got_ref[row, offset : offset + 32, :]) for row in range(16)], axis=0)
        return lax.dot_general(small_ref[2], tall, NT, preferred_element_type=F32)

    block = (amp_ref[...].astype(F32) + turned(0)).astype(BF16)
    for to in range(8):
        sent_ref[to] = block
    source = turned(32).astype(BF16)
    kept_ref[...] = lax.dot_general(source, wide_ref[...], NT, preferred_element_type=F32).astype(BF16)


def _gate_kernel(*refs):
    del refs


def _factor_kernel(fac0, fac1, fac2, fac3, halves_ref, rows_ref, right_ref, left_ref):
    y = lax.axis_index("y")
    for k, ref in enumerate((fac0, fac1, fac2, fac3)):
        for zh in range(4):
            part = _perm(halves_ref[...], ref[zh])
            right_ref[zh, (y + 4 - k) % 4] = jnp.concatenate([part[:64], part[64:]], axis=1)
    for x in range(4):
        rows = [right_ref[col // 4, col % 4, x * 16 : x * 16 + 16, :] for col in range(16)]
        part = _perm(rows_ref[...], jnp.concatenate(rows, axis=0))
        for zl in range(2):
            for core in range(2):
                at = zl * 128 + core * 64
                left_ref[x * 2 + zl, core] = part[at : at + 64]


def _second_step(left_ref, core, inner_ref, out_ref):
    for x in range(2):
        rows = jnp.concatenate([left_ref[x * 4 + chip, core] for chip in range(4)], axis=0)
        for j in range(4):
            cols = slice(j * 256, j * 256 + 256)
            part = _perm(rows, inner_ref[:, cols])
            for chip in range(4):
                out_ref[x * 4 + chip, :, cols] = part[chip * 64 : chip * 64 + 64]


def _first_step(amp_ref, right_ref, put):
    for i in range(2):
        rows = amp_ref[i * 4 : i * 4 + 4].reshape(256, 1024)
        for j in range(4):
            part = lax.dot_general(rows, right_ref[j].reshape(256, 1024), NT, preferred_element_type=F32)
            put(i, slice(j * 256, j * 256 + 256), part.astype(BF16))


def _own_kernel(own_ref, right_ref, part_ref):
    def put(i, cols, part):
        part_ref[i * 4 : i * 4 + 4, :, cols] = part.reshape(4, 64, 256)

    _first_step(own_ref, right_ref, put)


def _ladder_kernel(other_ref, right_ref, left_ref, part_ref, inner_ref, give_ref):
    core = lax.axis_index("core")
    first = core == 0

    def put(i, cols, part):
        for chip in range(4):
            own, other = part_ref[i * 4 + chip, :, cols], part[chip * 64 : chip * 64 + 64]
            at = (i * 4 + chip) * 128
            inner_ref[at : at + 64, cols] = jnp.where(first, own, other)
            inner_ref[at + 64 : at + 128, cols] = jnp.where(first, other, own)

    _first_step(other_ref, right_ref, put)
    _second_step(left_ref, 1 - core, inner_ref, give_ref)


def _rest_kernel(left_ref, inner_ref, keep_ref):
    _second_step(left_ref, lax.axis_index("core"), inner_ref, keep_ref)


def _sum_kernel(part_ref, kept_ref, small_ref, sent_ref):
    total = kept_ref[...].astype(F32)
    for chip in range(8):
        total += part_ref[chip].astype(F32)
    total = _perm(small_ref[1], total.astype(BF16))
    for col in range(16):
        sent_ref[col] = _pack(total[:, col * 64 : col * 64 + 64])


def _update_kernel(occ_ref, resid_ref, held_ref, mask_ref, vir_ref, out_ref, flat_ref):
    row = _chip() * 2 + lax.axis_index("core")
    col = lax.axis_index("zh") * 4 + lax.axis_index("y")
    exact = lax.Precision.HIGHEST

    def iota(shape, dim):
        return lax.broadcasted_iota(jnp.int32, shape, dim)

    mine = vir_ref[pl.ds(row // 2, 1), :]
    l_row = iota((32, 128), 1) - (row % 2) * 64
    in_row = (l_row // 2 == iota((32, 128), 0)) & (l_row >= 0)
    picked = jnp.where(in_row, jnp.broadcast_to(mine, (32, 128)), 0.0)
    same_half = (iota((128, 128), 0) % 2 == iota((128, 128), 1) // 64).astype(F32)
    vir_a = jnp.dot(picked, same_half, precision=exact, preferred_element_type=F32)
    lane = iota((128, 128), 1)
    want = ((lane // 4) % 2) * 64 + col * 4 + lane % 4
    choose = (iota((128, 128), 0) == want).astype(F32)
    by_block = jnp.dot(vir_ref[...], choose, precision=exact, preferred_element_type=F32)
    own_block = iota((8, 128), 0) == (iota((8, 128), 1) % 64) // 8
    vir_b = jnp.sum(jnp.where(own_block, by_block, 0.0), axis=0, keepdims=True)
    vir = vir_a + vir_b
    for pair in range(16):
        i, j = pair // 4, pair % 4
        denom = (occ_ref[i] + occ_ref[j]) - vir
        rsym = resid_ref[pair].astype(F32) + held_ref[pair, 32:].astype(F32)
        old = held_ref[pair, :32].astype(F32)
        flat_ref[pair * 32 : pair * 32 + 32, :] = old + mask_ref[pair : pair + 1, :] * (rsym / denom)
    for j in range(32):
        out_ref[:, j * 128 : (j + 1) * 128] = flat_ref[pl.ds(j, 16, stride=32), :].astype(BF16)


def _vmem():
    return pl.BlockSpec(memory_space=pltpu.VMEM)


SMEM = pl.BlockSpec(memory_space=pltpu.SMEM)
HBM = pl.BlockSpec(memory_space=pltpu.HBM)
ANY = pl.BlockSpec(memory_space=pl.ANY)


def _sds(*shape, dtype=BF16):
    return jax.ShapeDtypeStruct(shape, dtype)


def _turn(value, axis, step):
    if step == 0:
        return value
    return lax.ppermute(value, axis, [(i, (i + step) % 4) for i in range(4)])


def _swap_cores(value):
    return lax.ppermute(value, "core", [(0, 1), (1, 0)])


def _shards(tables, amps, source, factors, screen, occ_energy, vir_energy):
    small, wide, rows_b, halves = tables
    spread = pl.pallas_call(
        _spread_kernel,
        out_shape=_sds(64, 8, 512),
        in_specs=[_vmem()],
        out_specs=HBM,
        scratch_shapes=[pltpu.VMEM((16, 8, 512), F32), pltpu.VMEM((16, 8, 512), BF16)]
        + [pltpu.SemaphoreType.DMA((4,))],
        name="spread_factors",
    )(factors)
    fac = lax.all_to_all(spread, ("zh",) + ROWS, 0, 0, tiled=True).reshape(4, 128, 512)
    four = _sds(4, 96, 128)
    held, mask, *outs = pl.pallas_call(
        _mask_kernel,
        out_shape=(_sds(16, 64, 128), _sds(16, 128, dtype=F32)) + (four,) * 4,
        in_specs=[_vmem()] * 3,
        out_specs=(_vmem(),) * 6,
        scratch_shapes=[pltpu.VMEM((544, 128), F32)] * 2,
        name="mask_amps",
    )(amps.reshape(16, 4096), source.reshape(16, 4096), screen.transpose(1, 2, 0))
    outs = [_turn(out, "y", k) for k, out in enumerate(outs)]
    outs = pl.pallas_call(
        _relay_kernel,
        out_shape=(four,) * 4,
        in_specs=[_vmem()] * 4,
        out_specs=(_vmem(),) * 4,
        name="relay",
    )(*outs)
    outs = [_turn(out, "zh", k) for k, out in enumerate(outs)]
    near, far = _turn(fac, "y", 1), _turn(fac, "y", 3)
    opposite = _turn(fac, "y", 2)
    block, turn = pl.pallas_call(
        _block_kernel,
        out_shape=(_sds(64, 1024), _sds(16, 64, 128)),
        in_specs=[_vmem()] * 6,
        out_specs=(_vmem(), _vmem()),
        scratch_shapes=[pltpu.VMEM((4, 4, 96, 128), BF16)],
        compiler_params=VMEM,
        name="make_block",
    )(*outs, small, wide)
    turn = lax.all_to_all(turn, ROWS, 0, 0, tiled=True)
    block, kept = pl.pallas_call(
        _symmetric_kernel,
        out_shape=(_sds(8, 64, 1024), _sds(64, 1024)),
        in_specs=[_vmem()] * 4,
        out_specs=(_vmem(), _vmem()),
        compiler_params=VMEM,
        name="symmetrize",
    )(turn, block, small, wide)
    block = pl.pallas_call(
        _gate_kernel,
        out_shape=_sds(8, 64, 1024),
        in_specs=[_vmem()] + [ANY] * 3,
        out_specs=_vmem(),
        input_output_aliases={0: 0},
        compiler_params=VMEM,
        name="gate",
    )(block, near, far, opposite)
    own = lax.all_to_all(block, CHIPS, 0, 0, tiled=True)
    other = _swap_cores(own)
    right, left = pl.pallas_call(
        _factor_kernel,
        out_shape=(_sds(4, 4, 64, 1024), _sds(8, 2, 64, 1024)),
        in_specs=[_vmem()] * 6,
        out_specs=(_vmem(), _vmem()),
        compiler_params=VMEM,
        name="prepare_factors",
    )(fac, near, opposite, far, halves, rows_b)
    part = pl.pallas_call(
        _own_kernel,
        out_shape=_sds(8, 64, 1024),
        in_specs=[_vmem()] * 2,
        out_specs=_vmem(),
        compiler_params=VMEM,
        name="ladder_own",
    )(own, right)
    inner, give = pl.pallas_call(
        _ladder_kernel,
        out_shape=(_sds(1024, 1024), _sds(8, 64, 1024)),
        in_specs=[_vmem()] * 4,
        out_specs=(_vmem(), _vmem()),
        compiler_params=VMEM,
        name="ladder",
    )(other, right, left, part)
    keep = pl.pallas_call(
        _rest_kernel,
        out_shape=_sds(8, 64, 1024),
        in_specs=[_vmem()] * 2,
        out_specs=_vmem(),
        compiler_params=VMEM,
        name="ladder_rest",
    )(left, inner)
    taken = _swap_cores(give)
    partial = (keep.astype(F32) + taken.astype(F32)).astype(BF16)
    parts = lax.all_to_all(partial, CHIPS, 0, 0, tiled=True)
    last = pl.pallas_call(
        _sum_kernel,
        out_shape=_sds(16, 32, 128),
        in_specs=[_vmem()] * 3,
        out_specs=_vmem(),
        compiler_params=VMEM,
        name="sum_parts",
    )(parts, kept, small)
    back = lax.all_to_all(last, COLS, 0, 0, tiled=True)
    out = pl.pallas_call(
        _update_kernel,
        out_shape=_sds(16, 4096),
        in_specs=[SMEM, _vmem(), _vmem(), _vmem(), _vmem()],
        out_specs=_vmem(),
        scratch_shapes=[pltpu.VMEM((544, 128), F32)],
        name="update",
    )(occ_energy, back, held, mask, vir_energy.reshape(8, 128))
    return out.reshape(1, 1, 16, 4096)


def solution(mesh):
    fine = Mesh(mesh.devices.reshape(4, 2, 2, 4, 4), AXES)
    in_specs = (
        P(ROWS, COLS, None, None),
        P(ROWS, COLS, None, None),
        P(None, ROWS + COLS, None),
        P(),
        P(),
        P(),
    )
    shards = functools.partial(_shards, _tables())
    return jax.shard_map(shards, mesh=fine, in_specs=in_specs, out_specs=P(ROWS, COLS, None, None), check_vma=False)
```

```python
import functools

import jax
import jax.numpy as jnp
import numpy as np
from jax import lax
from jax.experimental import pallas as pl
from jax.experimental.pallas import tpu as pltpu
from jax.sharding import Mesh
from jax.sharding import PartitionSpec as P

AXES = ("x", "zl", "core", "zh", "y")
ROWS = ("x", "zl", "core")
COLS = ("zh", "y")
CHIPS = ("x", "zl")
VMEM = pltpu.CompilerParams(vmem_limit_bytes=40 * 1024 * 1024)
F32 = jnp.float32
BF16 = jnp.bfloat16
NT = (((1,), (1,)), ((), ()))
TN = (((0,), (0,)), ((), ()))


def _one_hot(source_of):
    source_of = np.asarray(source_of).reshape(-1)
    size = source_of.size
    out = np.zeros((size, size), np.float32)
    out[np.arange(size), source_of] = 1
    return out


def _grid(*sizes):
    return np.meshgrid(*[np.arange(s) for s in sizes], indexing="ij")


def _tables():
    j, h = _grid(32, 2)
    rows = _one_hot(h * 32 + j)
    small = np.stack([rows, rows.T, np.eye(64, dtype=np.float32)])
    row, col, k = _grid(16, 16, 4)
    wide = _one_hot(col * 64 + row * 4 + k).T
    row, col, k = _grid(4, 16, 4)
    rows_b = _one_hot(col * 16 + row * 4 + k)
    h, row, k = _grid(2, 16, 4)
    halves = _one_hot((row * 2 + h) * 4 + k)
    return [np.asarray(t, jnp.bfloat16) for t in (small, wide, rows_b, halves)]


def _chip():
    return lax.axis_index("x") * 2 + lax.axis_index("zl")


def _perm(left, right):
    return jnp.dot(left, right, preferred_element_type=F32).astype(BF16)


def _unpack(part):
    return jnp.concatenate([part[:, :64], part[:, 64:]], axis=0)


def _pack(piece):
    return jnp.concatenate([piece[:32], piece[32:]], axis=1)


def _spread_kernel(fac_ref, out_ref, wide_ref, send_ref, sems):
    wide_ref[:, :4, :] = fac_ref[:, :, :512].astype(F32)
    wide_ref[:, 4:, :] = fac_ref[:, :, 512:].astype(F32)
    send_ref[...] = wide_ref[...].astype(BF16)
    copies = [pltpu.make_async_copy(send_ref, out_ref.at[k * 16 : k * 16 + 16], sems.at[k]) for k in range(4)]
    for copy in copies:
        copy.start()
    for copy in copies:
        copy.wait()


def _virtuals(vir_ref):
    row = _chip() * 2 + lax.axis_index("core")
    col = lax.axis_index("zh") * 4 + lax.axis_index("y")
    exact = lax.Precision.HIGHEST

    def iota(shape, dim):
        return lax.broadcasted_iota(jnp.int32, shape, dim)

    mine = vir_ref[pl.ds(row // 2, 1), :]
    l_row = iota((32, 128), 1) - (row % 2) * 64
    in_row = (l_row // 2 == iota((32, 128), 0)) & (l_row >= 0)
    picked = jnp.where(in_row, jnp.broadcast_to(mine, (32, 128)), 0.0)
    same_half = (iota((128, 128), 0) % 2 == iota((128, 128), 1) // 64).astype(F32)
    vir_a = jnp.dot(picked, same_half, precision=exact, preferred_element_type=F32)
    lane = iota((128, 128), 1)
    want = ((lane // 4) % 2) * 64 + col * 4 + lane % 4
    choose = (iota((128, 128), 0) == want).astype(F32)
    by_block = jnp.dot(vir_ref[...], choose, precision=exact, preferred_element_type=F32)
    own_block = iota((8, 128), 0) == (iota((8, 128), 1) % 64) // 8
    vir_b = jnp.sum(jnp.where(own_block, by_block, 0.0), axis=0, keepdims=True)
    return vir_a + vir_b


def _mask_kernel(
    amps_ref,
    source_ref,
    screen_ref, vir_ref,
    held_ref,
    mask_ref, table_ref,
    out0,
    out1,
    out2,
    out3,
    flat_ref,
    flat2_ref,
):
    table_ref[...] = _virtuals(vir_ref)
    block = screen_ref[_chip()].astype(F32)
    lane_block = (lax.broadcasted_iota(jnp.int32, (8, 128), 1) % 64) // 8
    spread = (lax.broadcasted_iota(jnp.int32, (8, 128), 0) == lane_block).astype(F32)
    mask = lax.dot_general(block, spread, TN, preferred_element_type=F32)
    mask_ref[...] = mask
    y = lax.axis_index("y")
    for j in range(32):
        tile = slice(j * 128, (j + 1) * 128)
        flat_ref[pl.ds(j, 16, stride=32), :] = amps_ref[:, tile].astype(F32) * mask
        flat2_ref[pl.ds(j, 16, stride=32), :] = source_ref[:, tile].astype(F32)
    for pair in range(16):
        held_ref[pair, :32] = flat_ref[pair * 32 : pair * 32 + 32, :].astype(BF16)
        held_ref[pair, 32:] = flat2_ref[pair * 32 : pair * 32 + 32, :].astype(BF16)
    for k, out in enumerate((out0, out1, out2, out3)):
        to = (y + k) % 4
        for zh in range(4):
            rows = pl.ds(pl.multiple_of(zh * 128 + to * 32, 32), 32)
            turned = pl.ds(pl.multiple_of(to * 128 + zh * 32, 32), 32)
            out[zh, :32, :] = flat_ref[rows, :].astype(BF16)
            out[zh, 32:64, :] = flat_ref[turned, :].astype(BF16)
            out[zh, 64:, :] = flat2_ref[turned, :].astype(BF16)


def _relay_kernel(in0, in1, in2, in3, out0, out1, out2, out3):
    zh, y = lax.axis_index("zh"), lax.axis_index("y")
    for m, out in enumerate((out0, out1, out2, out3)):
        for k, ref in enumerate((in0, in1, in2, in3)):
            out[(y + 4 - k) % 4] = ref[(zh + m) % 4]


def _block_kernel(in0, in1, in2, in3, small_ref, wide_ref, amp_ref, sent_ref, got_ref):
    zh = lax.axis_index("zh")
    for m, ref in enumerate((in0, in1, in2, in3)):
        got_ref[(zh + 4 - m) % 4] = ref[...]

    def block(offset):
        parts = [_unpack(got_ref[c // 4, c % 4, offset : offset + 32, :]) for c in range(16)]
        return _perm(small_ref[0], jnp.concatenate(parts, axis=1))

    whole = jnp.concatenate([block(0), block(32), block(64)], axis=0)
    whole = _perm(whole, wide_ref[...])
    amp_ref[...] = whole[:64]
    for row in range(16):
        cols = slice(row * 64, row * 64 + 64)
        sent_ref[row, :32, :] = _pack(whole[64:128, cols])
        sent_ref[row, 32:, :] = _pack(whole[128:, cols])


def _symmetric_kernel(got_ref, amp_ref, small_ref, wide_ref, sent_ref, kept_ref):

    def turned(offset):
        tall = jnp.concatenate([_unpack(got_ref[row, offset : offset + 32, :]) for row in range(16)], axis=0)
        return lax.dot_general(small_ref[2], tall, NT, preferred_element_type=F32)

    block = (amp_ref[...].astype(F32) + turned(0)).astype(BF16)
    for to in range(8):
        sent_ref[to] = block
    source = turned(32).astype(BF16)
    kept_ref[...] = lax.dot_general(source, wide_ref[...], NT, preferred_element_type=F32).astype(BF16)


def _gate_kernel(*refs):
    del refs


def _factor_kernel(fac0, fac1, fac2, fac3, halves_ref, rows_ref, right_ref, left_ref):
    y = lax.axis_index("y")
    for k, ref in enumerate((fac0, fac1, fac2, fac3)):
        for zh in range(4):
            part = _perm(halves_ref[...], ref[zh])
            right_ref[zh, (y + 4 - k) % 4] = jnp.concatenate([part[:64], part[64:]], axis=1)
    for x in range(4):
        rows = [right_ref[col // 4, col % 4, x * 16 : x * 16 + 16, :] for col in range(16)]
        part = _perm(rows_ref[...], jnp.concatenate(rows, axis=0))
        for zl in range(2):
            for core in range(2):
                at = zl * 128 + core * 64
                left_ref[x * 2 + zl, core] = part[at : at + 64]


def _second_step(left_ref, core, inner_ref, out_ref, halves):
    for at, x in enumerate(halves):
        rows = jnp.concatenate([left_ref[x * 4 + chip, core] for chip in range(4)], axis=0)
        for j in range(4):
            cols = slice(j * 256, j * 256 + 256)
            part = _perm(rows, inner_ref[:, cols])
            for chip in range(4):
                out_ref[at * 4 + chip, :, cols] = part[chip * 64 : chip * 64 + 64]


def _first_step(amp_ref, right_ref, put):
    for i in range(2):
        rows = amp_ref[i * 4 : i * 4 + 4].reshape(256, 1024)
        for j in range(4):
            part = lax.dot_general(rows, right_ref[j].reshape(256, 1024), NT, preferred_element_type=F32)
            put(i, slice(j * 256, j * 256 + 256), part.astype(BF16))


def _own_kernel(own_ref, right_ref, part_ref):
    def put(i, cols, part):
        part_ref[i * 4 : i * 4 + 4, :, cols] = part.reshape(4, 64, 256)

    _first_step(own_ref, right_ref, put)


def _ladder_kernel(other_ref, right_ref, left_ref, part_ref, inner_ref, give_ref):
    core = lax.axis_index("core")
    first = core == 0

    def put(i, cols, part):
        for chip in range(4):
            own, other = part_ref[i * 4 + chip, :, cols], part[chip * 64 : chip * 64 + 64]
            at = (i * 4 + chip) * 128
            inner_ref[at : at + 64, cols] = jnp.where(first, own, other)
            inner_ref[at + 64 : at + 128, cols] = jnp.where(first, other, own)

    _first_step(other_ref, right_ref, put)
    _second_step(left_ref, 1 - core, inner_ref, give_ref, (0,))


def _more_kernel(left_ref, inner_ref, give_ref):
    _second_step(left_ref, 1 - lax.axis_index("core"), inner_ref, give_ref, (1,))


def _rest_kernel(left_ref, inner_ref, keep_ref):
    _second_step(left_ref, lax.axis_index("core"), inner_ref, keep_ref, (0, 1))


def _sum_kernel(part_ref, kept_ref, small_ref, sent_ref):
    total = kept_ref[...].astype(F32)
    for chip in range(8):
        total += part_ref[chip].astype(F32)
    total = _perm(small_ref[1], total.astype(BF16))
    for col in range(16):
        sent_ref[col] = _pack(total[:, col * 64 : col * 64 + 64])


def _update_kernel(occ_ref, resid_ref, held_ref, mask_ref, vir_ref, out_ref, flat_ref):
    for pair in range(16):
        i, j = pair // 4, pair % 4
        denom = (occ_ref[i] + occ_ref[j]) - vir_ref[...]
        rsym = resid_ref[pair].astype(F32) + held_ref[pair, 32:].astype(F32)
        old = held_ref[pair, :32].astype(F32)
        flat_ref[pair * 32 : pair * 32 + 32, :] = old + mask_ref[pair : pair + 1, :] * (rsym / denom)
    for j in range(32):
        out_ref[:, j * 128 : (j + 1) * 128] = flat_ref[pl.ds(j, 16, stride=32), :].astype(BF16)


def _vmem():
    return pl.BlockSpec(memory_space=pltpu.VMEM)


SMEM = pl.BlockSpec(memory_space=pltpu.SMEM)
HBM = pl.BlockSpec(memory_space=pltpu.HBM)
ANY = pl.BlockSpec(memory_space=pl.ANY)


def _sds(*shape, dtype=BF16):
    return jax.ShapeDtypeStruct(shape, dtype)


def _turn(value, axis, step):
    if step == 0:
        return value
    return lax.ppermute(value, axis, [(i, (i + step) % 4) for i in range(4)])


def _swap_cores(value):
    return lax.ppermute(value, "core", [(0, 1), (1, 0)])


def _shards(tables, amps, source, factors, screen, occ_energy, vir_energy):
    small, wide, rows_b, halves = tables
    spread = pl.pallas_call(
        _spread_kernel,
        out_shape=_sds(64, 8, 512),
        in_specs=[_vmem()],
        out_specs=HBM,
        scratch_shapes=[pltpu.VMEM((16, 8, 512), F32), pltpu.VMEM((16, 8, 512), BF16)]
        + [pltpu.SemaphoreType.DMA((4,))],
        name="spread_factors",
    )(factors)
    fac = lax.all_to_all(spread, ("zh",) + ROWS, 0, 0, tiled=True).reshape(4, 128, 512)
    four = _sds(4, 96, 128)
    held, mask, table, *outs = pl.pallas_call(
        _mask_kernel,
        out_shape=(_sds(16, 64, 128), _sds(16, 128, dtype=F32), _sds(32, 128, dtype=F32)) + (four,) * 4,
        in_specs=[_vmem()] * 4,
        out_specs=(_vmem(),) * 7,
        scratch_shapes=[pltpu.VMEM((544, 128), F32)] * 2,
        name="mask_amps",
    )(amps.reshape(16, 4096), source.reshape(16, 4096), screen.transpose(1, 2, 0), vir_energy.reshape(8, 128))
    outs = [_turn(out, "y", k) for k, out in enumerate(outs)]
    outs = pl.pallas_call(
        _relay_kernel,
        out_shape=(four,) * 4,
        in_specs=[_vmem()] * 4,
        out_specs=(_vmem(),) * 4,
        name="relay",
    )(*outs)
    outs = [_turn(out, "zh", k) for k, out in enumerate(outs)]
    near, far = _turn(fac, "y", 1), _turn(fac, "y", 3)
    opposite = _turn(fac, "y", 2)
    block, turn = pl.pallas_call(
        _block_kernel,
        out_shape=(_sds(64, 1024), _sds(16, 64, 128)),
        in_specs=[_vmem()] * 6,
        out_specs=(_vmem(), _vmem()),
        scratch_shapes=[pltpu.VMEM((4, 4, 96, 128), BF16)],
        compiler_params=VMEM,
        name="make_block",
    )(*outs, small, wide)
    turn = lax.all_to_all(turn, ROWS, 0, 0, tiled=True)
    block, kept = pl.pallas_call(
        _symmetric_kernel,
        out_shape=(_sds(8, 64, 1024), _sds(64, 1024)),
        in_specs=[_vmem()] * 4,
        out_specs=(_vmem(), _vmem()),
        compiler_params=VMEM,
        name="symmetrize",
    )(turn, block, small, wide)
    block = pl.pallas_call(
        _gate_kernel,
        out_shape=_sds(8, 64, 1024),
        in_specs=[_vmem()] + [ANY] * 3,
        out_specs=_vmem(),
        input_output_aliases={0: 0},
        compiler_params=VMEM,
        name="gate",
    )(block, near, far, opposite)
    own = lax.all_to_all(block, CHIPS, 0, 0, tiled=True)
    other = _swap_cores(own)
    right, left = pl.pallas_call(
        _factor_kernel,
        out_shape=(_sds(4, 4, 64, 1024), _sds(8, 2, 64, 1024)),
        in_specs=[_vmem()] * 6,
        out_specs=(_vmem(), _vmem()),
        compiler_params=VMEM,
        name="prepare_factors",
    )(fac, near, opposite, far, halves, rows_b)
    part = pl.pallas_call(
        _own_kernel,
        out_shape=_sds(8, 64, 1024),
        in_specs=[_vmem()] * 2,
        out_specs=_vmem(),
        compiler_params=VMEM,
        name="ladder_own",
    )(own, right)
    inner, give = pl.pallas_call(
        _ladder_kernel,
        out_shape=(_sds(1024, 1024), _sds(4, 64, 1024)),
        in_specs=[_vmem()] * 4,
        out_specs=(_vmem(), _vmem()),
        compiler_params=VMEM,
        name="ladder",
    )(other, right, left, part)
    more = pl.pallas_call(
        _more_kernel,
        out_shape=_sds(4, 64, 1024),
        in_specs=[_vmem()] * 2,
        out_specs=_vmem(),
        compiler_params=VMEM,
        name="ladder_more",
    )(left, inner)
    keep = pl.pallas_call(
        _rest_kernel,
        out_shape=_sds(8, 64, 1024),
        in_specs=[_vmem()] * 2,
        out_specs=_vmem(),
        compiler_params=VMEM,
        name="ladder_rest",
    )(left, inner)
    taken = jnp.concatenate([_swap_cores(give), _swap_cores(more)], axis=0)
    partial = (keep.astype(F32) + taken.astype(F32)).astype(BF16)
    parts = lax.all_to_all(partial, CHIPS, 0, 0, tiled=True)
    last = pl.pallas_call(
        _sum_kernel,
        out_shape=_sds(16, 32, 128),
        in_specs=[_vmem()] * 3,
        out_specs=_vmem(),
        compiler_params=VMEM,
        name="sum_parts",
    )(parts, kept, small)
    back = lax.all_to_all(last, COLS, 0, 0, tiled=True)
    out = pl.pallas_call(
        _update_kernel,
        out_shape=_sds(16, 4096),
        in_specs=[SMEM, _vmem(), _vmem(), _vmem(), _vmem()],
        out_specs=_vmem(),
        scratch_shapes=[pltpu.VMEM((544, 128), F32)],
        name="update",
    )(occ_energy, back, held, mask, table)
    return out.reshape(1, 1, 16, 4096)


def solution(mesh):
    fine = Mesh(mesh.devices.reshape(4, 2, 2, 4, 4), AXES)
    in_specs = (
        P(ROWS, COLS, None, None),
        P(ROWS, COLS, None, None),
        P(None, ROWS + COLS, None),
        P(),
        P(),
        P(),
    )
    shards = functools.partial(_shards, _tables())
    return jax.shard_map(shards, mesh=fine, in_specs=in_specs, out_specs=P(ROWS, COLS, None, None), check_vma=False)
```

```python
import functools

import jax
import jax.numpy as jnp
import numpy as np
from jax import lax
from jax.experimental import pallas as pl
from jax.experimental.pallas import tpu as pltpu
from jax.sharding import Mesh
from jax.sharding import PartitionSpec as P

AXES = ("x", "zl", "core", "zh", "y")
ROWS = ("x", "zl", "core")
COLS = ("zh", "y")
CHIPS = ("x", "zl")
VMEM = pltpu.CompilerParams(vmem_limit_bytes=40 * 1024 * 1024)
F32 = jnp.float32
BF16 = jnp.bfloat16
NT = (((1,), (1,)), ((), ()))
TN = (((0,), (0,)), ((), ()))


def _one_hot(source_of):
    source_of = np.asarray(source_of).reshape(-1)
    size = source_of.size
    out = np.zeros((size, size), np.float32)
    out[np.arange(size), source_of] = 1
    return out


def _grid(*sizes):
    return np.meshgrid(*[np.arange(s) for s in sizes], indexing="ij")


def _tables():
    j, h = _grid(32, 2)
    rows = _one_hot(h * 32 + j)
    small = np.stack([rows, rows.T, np.eye(64, dtype=np.float32)])
    row, col, k = _grid(16, 16, 4)
    wide = _one_hot(col * 64 + row * 4 + k).T
    row, col, k = _grid(4, 16, 4)
    rows_b = _one_hot(col * 16 + row * 4 + k)
    h, row, k = _grid(2, 16, 4)
    halves = _one_hot((row * 2 + h) * 4 + k)
    return [np.asarray(t, jnp.bfloat16) for t in (small, wide, rows_b, halves)]


def _chip():
    return lax.axis_index("x") * 2 + lax.axis_index("zl")


def _perm(left, right):
    return jnp.dot(left, right, preferred_element_type=F32).astype(BF16)


def _unpack(part):
    return jnp.concatenate([part[:, :64], part[:, 64:]], axis=0)


def _pack(piece):
    return jnp.concatenate([piece[:32], piece[32:]], axis=1)


def _spread_kernel(fac_ref, out_ref, wide_ref, send_ref, sems):
    wide_ref[:, :4, :] = fac_ref[:, :, :512].astype(F32)
    wide_ref[:, 4:, :] = fac_ref[:, :, 512:].astype(F32)
    send_ref[...] = wide_ref[...].astype(BF16)
    copies = [pltpu.make_async_copy(send_ref, out_ref.at[k * 16 : k * 16 + 16], sems.at[k]) for k in range(4)]
    for copy in copies:
        copy.start()
    for copy in copies:
        copy.wait()


def _virtuals(vir_ref):
    row = _chip() * 2 + lax.axis_index("core")
    col = lax.axis_index("zh") * 4 + lax.axis_index("y")
    exact = lax.Precision.HIGHEST

    def iota(shape, dim):
        return lax.broadcasted_iota(jnp.int32, shape, dim)

    mine = vir_ref[pl.ds(row // 2, 1), :]
    l_row = iota((32, 128), 1) - (row % 2) * 64
    in_row = (l_row // 2 == iota((32, 128), 0)) & (l_row >= 0)
    picked = jnp.where(in_row, jnp.broadcast_to(mine, (32, 128)), 0.0)
    same_half = (iota((128, 128), 0) % 2 == iota((128, 128), 1) // 64).astype(F32)
    vir_a = jnp.dot(picked, same_half, precision=exact, preferred_element_type=F32)
    lane = iota((128, 128), 1)
    want = ((lane // 4) % 2) * 64 + col * 4 + lane % 4
    choose = (iota((128, 128), 0) == want).astype(F32)
    by_block = jnp.dot(vir_ref[...], choose, precision=exact, preferred_element_type=F32)
    own_block = iota((8, 128), 0) == (iota((8, 128), 1) % 64) // 8
    vir_b = jnp.sum(jnp.where(own_block, by_block, 0.0), axis=0, keepdims=True)
    return vir_a + vir_b


def _mask_kernel(
    amps_ref,
    source_ref,
    screen_ref, vir_ref,
    held_ref,
    mask_ref, table_ref,
    out0,
    out1,
    out2,
    out3,
    flat_ref,
    flat2_ref,
):
    table_ref[...] = _virtuals(vir_ref)
    block = screen_ref[_chip()].astype(F32)
    lane_block = (lax.broadcasted_iota(jnp.int32, (8, 128), 1) % 64) // 8
    spread = (lax.broadcasted_iota(jnp.int32, (8, 128), 0) == lane_block).astype(F32)
    mask = lax.dot_general(block, spread, TN, preferred_element_type=F32)
    mask_ref[...] = mask
    y = lax.axis_index("y")
    for j in range(32):
        tile = slice(j * 128, (j + 1) * 128)
        flat_ref[pl.ds(j, 16, stride=32), :] = amps_ref[:, tile].astype(F32) * mask
        flat2_ref[pl.ds(j, 16, stride=32), :] = source_ref[:, tile].astype(F32)
    for pair in range(16):
        held_ref[pair, :32] = flat_ref[pair * 32 : pair * 32 + 32, :].astype(BF16)
        held_ref[pair, 32:] = flat2_ref[pair * 32 : pair * 32 + 32, :].astype(BF16)
    for k, out in enumerate((out0, out1, out2, out3)):
        to = (y + k) % 4
        for zh in range(4):
            rows = pl.ds(pl.multiple_of(zh * 128 + to * 32, 32), 32)
            turned = pl.ds(pl.multiple_of(to * 128 + zh * 32, 32), 32)
            out[zh, :32, :] = flat_ref[rows, :].astype(BF16)
            out[zh, 32:64, :] = flat_ref[turned, :].astype(BF16)
            out[zh, 64:, :] = flat2_ref[turned, :].astype(BF16)


def _relay_kernel(in0, in1, in2, in3, out0, out1, out2, out3):
    zh, y = lax.axis_index("zh"), lax.axis_index("y")
    for m, out in enumerate((out0, out1, out2, out3)):
        for k, ref in enumerate((in0, in1, in2, in3)):
            out[(y + 4 - k) % 4] = ref[(zh + m) % 4]


def _block_kernel(in0, in1, in2, in3, small_ref, wide_ref, amp_ref, sent_ref, got_ref):
    zh = lax.axis_index("zh")
    for m, ref in enumerate((in0, in1, in2, in3)):
        got_ref[(zh + 4 - m) % 4] = ref[...]

    def block(offset):
        parts = [_unpack(got_ref[c // 4, c % 4, offset : offset + 32, :]) for c in range(16)]
        return _perm(small_ref[0], jnp.concatenate(parts, axis=1))

    whole = jnp.concatenate([block(0), block(32), block(64)], axis=0)
    whole = _perm(whole, wide_ref[...])
    amp_ref[...] = whole[:64]
    for row in range(16):
        cols = slice(row * 64, row * 64 + 64)
        sent_ref[row, :32, :] = _pack(whole[64:128, cols])
        sent_ref[row, 32:, :] = _pack(whole[128:, cols])


def _symmetric_kernel(got_ref, amp_ref, small_ref, wide_ref, sent_ref, kept_ref):

    def turned(offset):
        tall = jnp.concatenate([_unpack(got_ref[row, offset : offset + 32, :]) for row in range(16)], axis=0)
        return lax.dot_general(small_ref[2], tall, NT, preferred_element_type=F32)

    block = (amp_ref[...].astype(F32) + turned(0)).astype(BF16)
    for to in range(8):
        sent_ref[to] = block
    source = turned(32).astype(BF16)
    kept_ref[...] = lax.dot_general(source, wide_ref[...], NT, preferred_element_type=F32).astype(BF16)


def _gate_kernel(*refs):
    del refs


def _factor_kernel(fac0, fac1, fac2, fac3, halves_ref, rows_ref, right_ref, left_ref):
    y = lax.axis_index("y")
    for k, ref in enumerate((fac0, fac1, fac2, fac3)):
        for zh in range(4):
            part = _perm(halves_ref[...], ref[zh])
            right_ref[zh, (y + 4 - k) % 4] = jnp.concatenate([part[:64], part[64:]], axis=1)
    for x in range(4):
        rows = [right_ref[col // 4, col % 4, x * 16 : x * 16 + 16, :] for col in range(16)]
        part = _perm(rows_ref[...], jnp.concatenate(rows, axis=0))
        for zl in range(2):
            for core in range(2):
                at = zl * 128 + core * 64
                left_ref[x * 2 + zl, core] = part[at : at + 64]


def _second_step(left_ref, core, inner_ref, out_ref):
    for x in range(2):
        rows = jnp.concatenate([left_ref[x * 4 + chip, core] for chip in range(4)], axis=0)
        for j in range(4):
            cols = slice(j * 256, j * 256 + 256)
            part = _perm(rows, inner_ref[:, cols])
            for chip in range(4):
                out_ref[x * 4 + chip, :, cols] = part[chip * 64 : chip * 64 + 64]


def _first_step(amp_ref, right_ref, put):
    for i in range(2):
        rows = amp_ref[i * 4 : i * 4 + 4].reshape(256, 1024)
        for j in range(4):
            part = lax.dot_general(rows, right_ref[j].reshape(256, 1024), NT, preferred_element_type=F32)
            put(i, slice(j * 256, j * 256 + 256), part.astype(BF16))


def _own_kernel(own_ref, right_ref, part_ref):
    def put(i, cols, part):
        part_ref[i * 4 : i * 4 + 4, :, cols] = part.reshape(4, 64, 256)

    _first_step(own_ref, right_ref, put)


def _ladder_kernel(other_ref, right_ref, left_ref, part_ref, inner_ref, give_ref):
    core = lax.axis_index("core")
    first = core == 0

    def put(i, cols, part):
        for chip in range(4):
            own, other = part_ref[i * 4 + chip, :, cols], part[chip * 64 : chip * 64 + 64]
            at = (i * 4 + chip) * 128
            inner_ref[at : at + 64, cols] = jnp.where(first, own, other)
            inner_ref[at + 64 : at + 128, cols] = jnp.where(first, other, own)

    _first_step(other_ref, right_ref, put)
    _second_step(left_ref, 1 - core, inner_ref, give_ref)


def _rest_kernel(left_ref, inner_ref, keep_ref):
    _second_step(left_ref, lax.axis_index("core"), inner_ref, keep_ref)


def _sum_kernel(part_ref, kept_ref, small_ref, sent_ref):
    total = kept_ref[...].astype(F32)
    for chip in range(8):
        total += part_ref[chip].astype(F32)
    total = _perm(small_ref[1], total.astype(BF16))
    for col in range(16):
        sent_ref[col] = _pack(total[:, col * 64 : col * 64 + 64])


def _update_kernel(occ_ref, resid_ref, held_ref, mask_ref, vir_ref, out_ref, flat_ref):
    for pair in range(16):
        i, j = pair // 4, pair % 4
        denom = (occ_ref[i] + occ_ref[j]) - vir_ref[...]
        rsym = resid_ref[pair].astype(F32) + held_ref[pair, 32:].astype(F32)
        old = held_ref[pair, :32].astype(F32)
        flat_ref[pair * 32 : pair * 32 + 32, :] = old + mask_ref[pair : pair + 1, :] * (rsym / denom)
    for j in range(32):
        out_ref[:, j * 128 : (j + 1) * 128] = flat_ref[pl.ds(j, 16, stride=32), :].astype(BF16)


def _vmem():
    return pl.BlockSpec(memory_space=pltpu.VMEM)


SMEM = pl.BlockSpec(memory_space=pltpu.SMEM)
HBM = pl.BlockSpec(memory_space=pltpu.HBM)
ANY = pl.BlockSpec(memory_space=pl.ANY)


def _sds(*shape, dtype=BF16):
    return jax.ShapeDtypeStruct(shape, dtype)


def _turn(value, axis, step):
    if step == 0:
        return value
    return lax.ppermute(value, axis, [(i, (i + step) % 4) for i in range(4)])


def _swap_cores(value):
    return lax.ppermute(value, "core", [(0, 1), (1, 0)])


def _shards(tables, amps, source, factors, screen, occ_energy, vir_energy):
    small, wide, rows_b, halves = tables
    spread = pl.pallas_call(
        _spread_kernel,
        out_shape=_sds(64, 8, 512),
        in_specs=[_vmem()],
        out_specs=HBM,
        scratch_shapes=[pltpu.VMEM((16, 8, 512), F32), pltpu.VMEM((16, 8, 512), BF16)]
        + [pltpu.SemaphoreType.DMA((4,))],
        name="spread_factors",
    )(factors)
    fac = lax.all_to_all(spread, ("zh",) + ROWS, 0, 0, tiled=True).reshape(4, 128, 512)
    four = _sds(4, 96, 128)
    held, mask, table, *outs = pl.pallas_call(
        _mask_kernel,
        out_shape=(_sds(16, 64, 128), _sds(16, 128, dtype=F32), _sds(32, 128, dtype=F32)) + (four,) * 4,
        in_specs=[_vmem()] * 4,
        out_specs=(_vmem(),) * 7,
        scratch_shapes=[pltpu.VMEM((544, 128), F32)] * 2,
        name="mask_amps",
    )(amps.reshape(16, 4096), source.reshape(16, 4096), screen.transpose(1, 2, 0), vir_energy.reshape(8, 128))
    outs = [_turn(out, "y", k) for k, out in enumerate(outs)]
    outs = pl.pallas_call(
        _relay_kernel,
        out_shape=(four,) * 4,
        in_specs=[_vmem()] * 4,
        out_specs=(_vmem(),) * 4,
        name="relay",
    )(*outs)
    outs = [_turn(out, "zh", k) for k, out in enumerate(outs)]
    near, far = _turn(fac, "y", 1), _turn(fac, "y", 3)
    opposite = _turn(fac, "y", 2)
    block, turn = pl.pallas_call(
        _block_kernel,
        out_shape=(_sds(64, 1024), _sds(16, 64, 128)),
        in_specs=[_vmem()] * 6,
        out_specs=(_vmem(), _vmem()),
        scratch_shapes=[pltpu.VMEM((4, 4, 96, 128), BF16)],
        compiler_params=VMEM,
        name="make_block",
    )(*outs, small, wide)
    turn = lax.all_to_all(turn, ROWS, 0, 0, tiled=True)
    block, kept = pl.pallas_call(
        _symmetric_kernel,
        out_shape=(_sds(8, 64, 1024), _sds(64, 1024)),
        in_specs=[_vmem()] * 4,
        out_specs=(_vmem(), _vmem()),
        compiler_params=VMEM,
        name="symmetrize",
    )(turn, block, small, wide)
    block = pl.pallas_call(
        _gate_kernel,
        out_shape=_sds(8, 64, 1024),
        in_specs=[_vmem()] + [ANY] * 3,
        out_specs=_vmem(),
        input_output_aliases={0: 0},
        compiler_params=VMEM,
        name="gate",
    )(block, near, far, opposite)
    own = lax.all_to_all(block, CHIPS, 0, 0, tiled=True)
    other = _swap_cores(own)
    right, left = pl.pallas_call(
        _factor_kernel,
        out_shape=(_sds(4, 4, 64, 1024), _sds(8, 2, 64, 1024)),
        in_specs=[_vmem()] * 6,
        out_specs=(_vmem(), _vmem()),
        compiler_params=VMEM,
        name="prepare_factors",
    )(fac, near, opposite, far, halves, rows_b)
    part = pl.pallas_call(
        _own_kernel,
        out_shape=_sds(8, 64, 1024),
        in_specs=[_vmem()] * 2,
        out_specs=_vmem(),
        compiler_params=VMEM,
        name="ladder_own",
    )(own, right)
    inner, give = pl.pallas_call(
        _ladder_kernel,
        out_shape=(_sds(1024, 1024), _sds(8, 64, 1024)),
        in_specs=[_vmem()] * 4,
        out_specs=(_vmem(), _vmem()),
        compiler_params=VMEM,
        name="ladder",
    )(other, right, left, part)
    keep = pl.pallas_call(
        _rest_kernel,
        out_shape=_sds(8, 64, 1024),
        in_specs=[_vmem()] * 2,
        out_specs=_vmem(),
        compiler_params=VMEM,
        name="ladder_rest",
    )(left, inner)
    taken = _swap_cores(give)
    partial = (keep.astype(F32) + taken.astype(F32)).astype(BF16)
    parts = lax.all_to_all(partial, CHIPS, 0, 0, tiled=True)
    last = pl.pallas_call(
        _sum_kernel,
        out_shape=_sds(16, 32, 128),
        in_specs=[_vmem()] * 3,
        out_specs=_vmem(),
        compiler_params=VMEM,
        name="sum_parts",
    )(parts, kept, small)
    back = lax.all_to_all(last, COLS, 0, 0, tiled=True)
    out = pl.pallas_call(
        _update_kernel,
        out_shape=_sds(16, 4096),
        in_specs=[SMEM, _vmem(), _vmem(), _vmem(), _vmem()],
        out_specs=_vmem(),
        scratch_shapes=[pltpu.VMEM((544, 128), F32)],
        name="update",
    )(occ_energy, back, held, mask, table)
    return out.reshape(1, 1, 16, 4096)


def solution(mesh):
    fine = Mesh(mesh.devices.reshape(4, 2, 2, 4, 4), AXES)
    in_specs = (
        P(ROWS, COLS, None, None),
        P(ROWS, COLS, None, None),
        P(None, ROWS + COLS, None),
        P(),
        P(),
        P(),
    )
    shards = functools.partial(_shards, _tables())
    return jax.shard_map(shards, mesh=fine, in_specs=in_specs, out_specs=P(ROWS, COLS, None, None), check_vma=False)
```
